128 devices in a mesh: elem: 8 (over y, core), col: 16 (over x, z).
Axes of the slice: x: 4, y: 4, z: 4, core: 2. Of those that a mesh axis runs over, the one named last changes fastest.
Arguments:
- absorbers: float32 [8, 64, 32768], P(None, None, ('elem', 'col')), may hold values from 0.2 to 5
- cloud_tau: float32 [14, 64, 32768], P(None, None, ('elem', 'col')), may hold values from 0.001 to 0.5
- cloud_ssa: float32 [14, 64, 32768], P(None, None, ('elem', 'col')), may hold values from 0.3 to 0.9
- cloud_asym: float32 [14, 64, 32768], P(None, None, ('elem', 'col')), may hold values from 0.5 to 0.9
- thickness: float32 [64, 32768], P(None, ('elem', 'col')), may hold values from 0.5 to 2
- coszen: float32 [32768], P(('elem', 'col')), may hold values from 0.15 to 1
- albedo: float32 [14, 32768], P(None, ('elem', 'col')), may hold values from 0.05 to 0.8
- sunlit: int32 [32768], P(('elem', 'col')), may hold values from 0 to 1, as said below
- slot_order: int32 [128, 256], P(('elem', 'col')), may hold values from 0 to 255, as said below
- kcoef: float32 [8, 64, 112], replicated, may hold values from 0.02 to 2
- solar: float32 [112], replicated, may hold values from 0.2 to 5
- band_of_g: int32 [112], replicated, may hold values from 0 to 13
Outputs:
- heating: float32 [64, 32768], P(None, ('elem', 'col'))
- surface_down: float32 [32768], P(('elem', 'col'))
The draws below stay inside these ranges and needn't reach their ends.
Inputs may be any that keep to these rules, and one draw needn't show every extreme that they name: `slot_order`: each row is a permutation of the owner's 256 columns; slot s sends its column to span device s // 2, which places it at d * 2 + s % 2 for owner d. In the span layout given by slot_order, the two span devices of one elem index whose col indices lie half the col axis apart hold exactly 256 sunlit columns together.
All inputs are finite; a program needn't handle non-finite values.
Results may differ from the reference program's by a relative error of at most 0.0003.
Values sent between devices are 32-bit elements; how exact they have to be, the bound alone decides.
A program may use at most 192 MiB of HBM per device.

```python
import math
import jax
import jax.numpy as jnp
from jax import lax

NG = 112
NBND = 14
NSP = 8
NLEV = 64
CH = 256
DEVS = 128
COLUMNS = 32768
BLK = 2
N_ELEM = 8
N_COL = 16


def layout_tables(key):
    key_first, key_second, key_third = jax.random.split(key, 3)
    inverse = jax.vmap(lambda item: jax.random.permutation(item, CH))(jax.random.split(key_first, DEVS)).astype(jnp.int32)
    owner = jnp.arange(DEVS, dtype=jnp.int32)[:, None]
    target = inverse // BLK
    position = owner * BLK + inverse % BLK
    pair_half = N_COL // 2
    day_count = jax.random.randint(key_second, (N_ELEM, pair_half), CH // 2, CH + 1).astype(jnp.int32)
    device = jnp.arange(DEVS, dtype=jnp.int32)
    column_index = device % N_COL
    paired = day_count[device // N_COL, column_index % pair_half]
    lit_count = jnp.where(column_index < pair_half, paired, CH - paired)
    ranking = jax.vmap(lambda item: jax.random.permutation(item, CH))(jax.random.split(key_third, DEVS)).astype(jnp.int32)
    lighted = (ranking[target, position] < lit_count[target]).astype(jnp.int32)
    return (inverse, lighted.reshape(DEVS * CH))


def draw_sunlit(key, part):
    return layout_tables(key)[1]


def draw_slot_order(key, part):
    inverse = layout_tables(key)[0]
    return jnp.argsort(inverse, axis=1).astype(jnp.int32)


def set_ends(drawn, rng, smallest, top_value):
    index_at = [jax.random.randint(jax.random.fold_in(rng, axis), (), 0, length) for axis, length in enumerate(drawn.shape)]
    main_axis = drawn.shape.index(max(drawn.shape))
    next_to = index_at[:main_axis] + [(index_at[main_axis] + 1) % drawn.shape[main_axis]] + index_at[main_axis + 1:]
    return drawn.at[tuple(index_at)].set(smallest).at[tuple(next_to)].set(top_value)


def shard_levels(rng, dims, cuts, smallest, high):
    gain = 1.0
    for dim, parts in cuts:
        heights = jax.random.uniform(jax.random.fold_in(jax.random.fold_in(rng, 6), dim), (parts,), jnp.float32, smallest / len(cuts), high / len(cuts))
        gain = gain * jnp.repeat(jnp.exp(heights), dims[dim] // parts).reshape((-1,) + (1,) * (len(dims) - 1 - dim))
    return gain


def setup_inputs(seed: int = 0) -> dict:
    arg_keys = jax.random.split(jax.random.key(seed), 13)
    return {
        "absorbers": jnp.clip(jnp.exp(math.log(5.0) - 3.218876 * jax.random.uniform(arg_keys[0], (NSP, NLEV, COLUMNS), jnp.float32) ** shard_levels(arg_keys[0], (NSP, NLEV, COLUMNS), ((2, 128),), -0.2, 0.2)), 0.2, 5.0),
        "cloud_tau": jnp.clip(jnp.exp(math.log(0.5) - 6.214608 * jax.random.uniform(arg_keys[1], (NBND, NLEV, COLUMNS), jnp.float32) ** shard_levels(arg_keys[1], (NBND, NLEV, COLUMNS), ((2, 128),), -0.2, 0.2)), 0.001, 0.5),
        "cloud_ssa": jnp.clip(0.3 + 0.59999996 * jax.random.uniform(arg_keys[2], (NBND, NLEV, COLUMNS), jnp.float32) ** shard_levels(arg_keys[2], (NBND, NLEV, COLUMNS), ((2, 128),), -0.2, 0.2), 0.3, 0.9),
        "cloud_asym": jnp.clip(0.5 + 0.39999998 * jax.random.uniform(arg_keys[3], (NBND, NLEV, COLUMNS), jnp.float32) ** shard_levels(arg_keys[3], (NBND, NLEV, COLUMNS), ((2, 128),), -0.2, 0.2), 0.5, 0.9),
        "thickness": jnp.clip(jnp.exp(math.log(2.0) - 1.3862944 * jax.random.uniform(arg_keys[4], (NLEV, COLUMNS), jnp.float32) ** shard_levels(arg_keys[4], (NLEV, COLUMNS), ((1, 128),), -0.2, 0.2)), 0.5, 2.0),
        "coszen": jnp.clip(0.15 + 0.85 * jax.random.uniform(arg_keys[5], (COLUMNS,), jnp.float32) ** shard_levels(arg_keys[5], (COLUMNS,), ((0, 128),), -0.2, 0.2), 0.15, 1.0),
        "albedo": jnp.clip(0.05 + 0.75 * jax.random.uniform(arg_keys[6], (NBND, COLUMNS), jnp.float32) ** shard_levels(arg_keys[6], (NBND, COLUMNS), ((1, 128),), -0.2, 0.2), 0.05, 0.8),
        "sunlit": draw_sunlit(jax.random.fold_in(arg_keys[12], 71), 0),
        "slot_order": draw_slot_order(jax.random.fold_in(arg_keys[12], 71), 0),
        "kcoef": jnp.clip(jnp.exp(jax.random.uniform(arg_keys[9], (NSP, NLEV, NG), jnp.float32, math.log(0.02), math.log(2.0))), 0.02, 2.0),
        "solar": jnp.clip(jnp.exp(jax.random.uniform(arg_keys[10], (NG,), jnp.float32, math.log(0.2), math.log(5.0))), 0.2, 5.0),
        "band_of_g": set_ends(jax.random.randint(arg_keys[11], (NG,), 0, NBND), jax.random.fold_in(arg_keys[11], 1), 0, NBND - 1).astype(jnp.int32),
    }


HIGHEST_PRECISION = lax.Precision.HIGHEST

def radiate(absorb, coef_slab, thickness, cloud_depth, cloud_single, cloud_forward, select, albedo, cosine_safe, weight_cosine):
    levels = thickness.shape[0]
    gas_depth = jnp.einsum('slg,slc->lgc', coef_slab, absorb, precision=HIGHEST_PRECISION) * (thickness[:, None, :] / levels)
    depth_cloud = jnp.einsum('gb,blc->lgc', select, cloud_depth, precision=HIGHEST_PRECISION)
    single_cloud = jnp.einsum('gb,blc->lgc', select, cloud_single, precision=HIGHEST_PRECISION)
    forward = jnp.einsum('gb,blc->lgc', select, cloud_forward, precision=HIGHEST_PRECISION)
    surface_albedo = jnp.dot(select, albedo, precision=HIGHEST_PRECISION)
    total_depth = gas_depth + depth_cloud
    single = single_cloud * depth_cloud / total_depth
    gamma_one = 2.0 - single * (1.0 + forward)
    gamma_two = single * (1.0 - forward)
    root_rate = jnp.sqrt((gamma_one - gamma_two) * (gamma_one + gamma_two))
    decay_one = jnp.exp(-root_rate * total_depth)
    decay_square = decay_one * decay_one
    denominator = root_rate * (1.0 + decay_square) + gamma_one * (1.0 - decay_square)
    reflect = gamma_two * (1.0 - decay_square) / denominator
    transmit = 2.0 * root_rate * decay_one / denominator
    unscattered = jnp.exp(-total_depth / cosine_safe)
    backward = 0.5 * (1.0 - forward * cosine_safe)
    scattered = (1.0 - unscattered) * single
    reflect_beam = scattered * backward
    transmit_beam = scattered * (1.0 - backward)

    def beam_step(beam_now, factor):
        return (beam_now * factor, beam_now)
    beam_bottom, beam_top = lax.scan(beam_step, jnp.ones(surface_albedo.shape, jnp.float32), unscattered)
    source_up = reflect_beam * beam_top
    source_down = transmit_beam * beam_top

    def climb_up(state, layer_terms):
        albedo_below, source_below = state
        r_layer, t_layer, s_up, s_down = layer_terms
        inverse = 1.0 / (1.0 - r_layer * albedo_below)
        albedo_above = r_layer + t_layer * t_layer * albedo_below * inverse
        source_above = s_up + t_layer * inverse * (source_below + albedo_below * s_down)
        return ((albedo_above, source_above), (albedo_below, source_below, inverse))
    (albedo_top, source_top), (albedo_low, source_low, inverse_all) = lax.scan(climb_up, (surface_albedo, surface_albedo * beam_bottom), (reflect, transmit, source_up, source_down), reverse=True)

    def descend(down_flux, layer_terms):
        r_layer, t_layer, s_down, a_below, q_below, inverse = layer_terms
        down_next = (t_layer * down_flux + r_layer * q_below + s_down) * inverse
        return (down_next, down_next - (a_below * down_next + q_below))
    down_bottom, diffuse_net = lax.scan(descend, jnp.zeros_like(surface_albedo), (reflect, transmit, source_down, albedo_low, source_low, inverse_all))
    net_top = 1.0 - source_top
    net_rest = beam_top * unscattered + diffuse_net
    net_flux = jnp.concatenate([net_top[None], net_rest], axis=0)
    net_sum = lax.optimization_barrier(jnp.sum(net_flux * weight_cosine[None], axis=1))
    surface = lax.optimization_barrier(jnp.sum(weight_cosine * (beam_bottom + down_bottom), axis=0))
    return (net_sum, surface)

def column_physics(absorb, cloud_depth, cloud_single, cloud_forward, thickness, cosine, albedo, kcoef, weight, select):
    levels = thickness.shape[0]
    cosine_safe = jnp.where(cosine > 0, cosine, 1.0)
    weight_cosine = weight[:, None] * cosine[None, :]
    net_total, surface = radiate(absorb, kcoef, thickness, cloud_depth, cloud_single, cloud_forward, select, albedo, cosine_safe, weight_cosine)
    heating = levels * (net_total[:-1] - net_total[1:]) / thickness
    return (heating, surface)

def reference(absorbers, cloud_tau, cloud_ssa, cloud_asym, thickness, coszen, albedo, sunlit, slot_order, kcoef, solar, band_of_g):
    cosine = jnp.where(sunlit == 1, coszen, 0.0)
    weight = solar / jnp.sum(solar)
    select = (band_of_g[:, None] == jnp.arange(NBND, dtype=jnp.int32)[None, :]).astype(jnp.float32)

    def blocked(array):
        shaped = array.reshape(array.shape[:-1] + (DEVS, CH))
        return jnp.moveaxis(shaped, -2, 0)

    def per_block(items):
        return column_physics(items[0], items[1], items[2], items[3], items[4], items[5], items[6], kcoef, weight, select)
    heat_blocks, surface_blocks = lax.map(per_block, (blocked(absorbers), blocked(cloud_tau), blocked(cloud_ssa), blocked(cloud_asym), blocked(thickness), blocked(cosine), blocked(albedo)))
    heating = jnp.moveaxis(heat_blocks, 0, 1).reshape(NLEV, DEVS * CH)
    slotted = jnp.take_along_axis(surface_blocks, slot_order.astype(jnp.int32), axis=1)
    surface_down = jnp.transpose(slotted.reshape(DEVS, DEVS, BLK), (1, 0, 2)).reshape(DEVS * CH)
    return (heating, surface_down)
```

```python
import functools
import math

import jax
import jax.numpy as jnp
from jax import lax
from jax.experimental import pallas as pl
from jax.experimental.pallas import tpu as pltpu
from jax.sharding import PartitionSpec as P

MESH = pl.DeviceIdType.MESH
F32 = jnp.float32
BF16 = jnp.bfloat16

NG = 112
NBND = 14
NSP = 8
NLEV = 64
CH = 256
N_ELEM = 8
N_COL = 16
DEVS = 128

WIDE = 128
NARROW = 32
MAIN = WIDE + NARROW
STARTS = (0, 32, 64, 88)
A_CHUNKS = NG // 8
B_CHUNKS = 4
SCALE = 2.0 * math.log2(math.e)


def dot(a, b):
    return jnp.dot(a, b, preferred_element_type=F32)


def iota(shape, axis):
    return lax.broadcasted_iota(jnp.int32, shape, axis)


def one(mask):
    return jnp.where(mask, 1.0, 0.0).astype(BF16)


def halves(x):
    hi = x.astype(BF16)
    return hi, (x - hi.astype(F32)).astype(BF16)


def thirds(x):
    hi = x.astype(BF16)
    rest = x - hi.astype(F32)
    mid = rest.astype(BF16)
    return hi, mid, (rest - mid.astype(F32)).astype(BF16)


def row_times(row, matrix):
    hi, mid, low = thirds(row)
    at = iota((16, row.shape[1]), 0)
    stack = jnp.where(at == 0, hi.astype(F32), jnp.where(at == 1, mid.astype(F32), jnp.where(at == 2, low.astype(F32), 0.0)))
    return jnp.sum(dot(stack.astype(BF16), matrix), axis=0, keepdims=True)


class Tile:
    def __init__(self, first, packed):
        self.first = first
        self.packed = packed
        self.lanes = 2 * WIDE if packed else WIDE
        self.chunks = A_CHUNKS + (B_CHUNKS if packed else 0)

    def compact(self, lane):
        return self.first + jnp.where(lane < WIDE, lane, WIDE + lane % NARROW)


def physics(tile, refs, scr, after_up=None, started=None):
    (ab, ct, cs, ca, th, mu, alb, sun, slot, kc, sol, band) = refs
    (rhs, kt, lhs, buf, state, coef, net, fl, albs) = scr
    lanes, chunks = tile.lanes, tile.chunks

    lit = jnp.where(sun[...] == 1, 1.0, 0.0)
    ri, ci = iota((CH, CH), 0), iota((CH, CH), 1)
    litb = jnp.broadcast_to(lit, (CH, CH))
    ones = jnp.ones((CH, CH), BF16)
    rank_c = dot(jnp.where(ci < ri, litb, 0.0).astype(BF16), ones[:, :lanes])
    lit_c = dot(jnp.where(ci == ri, litb, 0.0).astype(BF16), ones[:, :lanes])
    row_lit = jnp.broadcast_to(lit, (16, CH)).astype(BF16)
    rank_r = dot(row_lit, one(ri < ci))[0:1]
    count = dot(row_lit, ones)[0:1]
    want_c = tile.compact(iota((CH, lanes), 1)).astype(F32)
    gather = one(jnp.where(want_c >= count[:, :lanes], jnp.where(iota((CH, lanes), 0) == 0, 1.0, 0.0), jnp.where(rank_c == want_c, lit_c, 0.0)) > 0.5)
    want_r = tile.compact(iota((lanes, CH), 0)).astype(F32)
    spread = one(jnp.where(rank_r == want_r, jnp.broadcast_to(lit, (lanes, CH)), 0.0) > 0.5)
    to_slot = dot(spread, one(slot[...] == ri)).astype(BF16)

    eye = iota((NG, NG), 0) == iota((NG, NG), 1)
    solar = sol[...]
    weight = jnp.sum(jnp.where(eye, solar / jnp.sum(solar, axis=1, keepdims=True), 0.0), axis=1, keepdims=True)
    band_c = jnp.sum(jnp.where(eye, band[...].astype(F32), 0.0), axis=1, keepdims=True)
    k = iota((NG, CH), 1) % 128
    for l8 in range(8):
        pick = one((k // 8).astype(F32) == jnp.where(k % 8 == l8, band_c, -1.0))
        lhs[l8 // 4, (l8 % 4) * NG:(l8 % 4 + 1) * NG, 256:512] = pick
    for grp in range(8):
        rows = jnp.concatenate([kc[s, 8 * grp:8 * grp + 8, :] for s in range(NSP)], axis=0)
        hi = rows.astype(BF16).astype(F32)
        low = rows - hi
        kt[grp, :, 0:128] = jnp.concatenate([hi, hi], axis=0).T.astype(BF16)
        kt[grp, :, 128:256] = jnp.concatenate([low, low], axis=0).T.astype(BF16)

    quarter = iota((8, WIDE), 1) // NARROW

    def pack(get, j):
        if j == 3:
            return jnp.where(quarter == 0, get(24), get(56))
        v = [get(s + 8 * j) for s in STARTS]
        return jnp.where(quarter == 0, v[0], jnp.where(quarter == 1, v[1], jnp.where(quarter == 2, v[2], v[3])))

    a_hi, a_low = halves(jnp.concatenate([alb[...], jnp.zeros((2, CH), F32)], axis=0))
    zero = jnp.zeros((112, lanes), BF16)
    a_rhs = jnp.concatenate([dot(a_hi, gather).astype(BF16), zero, dot(a_low, gather).astype(BF16), zero], axis=0)
    albs[...] = dot(one(k.astype(F32) == band_c), a_rhs)
    cosine = mu[...]
    cos = row_times(cosine, gather)
    cos_safe = jnp.where(cos > 0, cos, 1.0)
    rate = -0.5 / cos_safe
    wfull = jnp.broadcast_to(weight, (NG, WIDE))

    def lanes_of(x, c):
        return x[:, :WIDE] if c < A_CHUNKS else x[:, WIDE:]

    def chunk_of(c, get):
        if c < A_CHUNKS:
            return get(8 * c, 0)
        return pack(lambda row: get(row, WIDE), c - A_CHUNKS)

    def beam_top(c):
        w = chunk_of(c, lambda row, lane: wfull[row:row + 8])
        if c == A_CHUNKS + 3:
            w = jnp.where(quarter < 2, w, 0.0)
        return w * lanes_of(cos, c)

    for c in range(chunks):
        a = chunk_of(c, lambda row, lane: albs[row:row + 8, lane:lane + WIDE])
        at = slice(8 * c, 8 * c + 8)
        state[0, at] = a
        state[1, at] = a
        state[2, at] = jnp.ones((8, WIDE), F32)
        state[3, at] = jnp.ones((8, WIDE), F32)

    def prepare(grp, _):
        rows = pl.ds(pl.multiple_of(grp * 8, 8), 8)
        thick = th[rows, :] * (SCALE / NLEV)
        gas = (ab[:, rows, :] * thick[None]).reshape(64, CH)
        tau = (ct[:, rows, :] * SCALE).reshape(112, CH)
        tau_s = tau * cs[:, rows, :].reshape(112, CH)
        tau_f = tau_s * ca[:, rows, :].reshape(112, CH)
        hi, low = halves(jnp.concatenate([gas, tau, tau_s, tau_f], axis=0))
        hi = dot(hi, gather).astype(BF16)
        low = dot(low, gather).astype(BF16)
        rhs[grp, 0:64] = hi[0:64]
        rhs[grp, 64:128] = low[0:64]
        rhs[grp, 128:192] = hi[0:64]
        rhs[grp, 192:256] = low[0:64]
        gap = jnp.zeros((16, lanes), BF16)
        for i in range(3):
            at = 64 + 112 * i
            rhs[grp, 256 * i + 256:256 * i + 368] = hi[at:at + 112]
            rhs[grp, 256 * i + 368:256 * i + 384] = gap
            rhs[grp, 256 * i + 384:256 * i + 496] = low[at:at + 112]
            rhs[grp, 256 * i + 496:256 * i + 512] = gap
        return 0

    lax.fori_loop(0, 8, prepare, 0)

    lane8 = iota((NG, CH), 1) % 8

    def optics(grp, hf):
        for j in range(4):
            lhs[hf, j * NG:(j + 1) * NG, 0:256] = jnp.where(lane8 == hf * 4 + j, kt[grp].astype(F32), 0.0).astype(BF16)
        buf[hf, 0] = dot(lhs[hf], rhs[grp, 0:512])
        buf[hf, 1] = dot(lhs[hf, :, 256:512], rhs[grp, 512:768])
        buf[hf, 2] = dot(lhs[hf, :, 256:512], rhs[grp, 768:1024])

    def climb(grp, hf):
        for c in range(chunks):
            at = slice(8 * c, 8 * c + 8)
            a, q, tt, sb = (state[i, at] for i in range(4))
            m, r = lanes_of(cos_safe, c), lanes_of(rate, c)
            for j in (3, 2, 1, 0):
                t, s, f = (chunk_of(c, lambda row, lane: buf[hf, i, j * NG + row:j * NG + row + 8, lane:lane + WIDE]) for i in range(3))
                p1 = t - s
                p2 = t - f
                pp = p1 * p2
                kk = pp * lax.rsqrt(pp)
                e = jnp.exp2(-kk)
                e2 = e * e
                tot = p1 + p2
                k2 = kk + kk
                inv_d = pl.reciprocal((tot + k2) - e2 * (tot - k2), approx=True)
                rdif = (s - f) * (1.0 - e2) * inv_d
                tdif = (k2 + k2) * e * inv_d
                u = jnp.exp2(t * r)
                sc = (1.0 - u) * pl.reciprocal(t + t, approx=True)
                mf = m * f
                rdir = sc * (s - mf)
                tdir = sc * (s + mf)
                inv = pl.reciprocal(1.0 - rdif * a, approx=True)
                ti = tdif * inv
                qu = q * u
                b = (rdif * qu + tdir) * inv
                level = pl.multiple_of((grp * 8 + hf * 4 + j) * (8 * chunks), 8) + 8 * c
                w = pl.ds(pl.multiple_of(level, 8), 8)
                coef[0, w] = ti
                coef[1, w] = b
                coef[2, w] = u
                coef[3, w] = 1.0 - a
                coef[4, w] = 1.0 - q
                sb = tt * b + sb * u
                tt = tt * ti
                q = rdir + ti * (qu + a * tdir)
                a = rdif + tdif * (a * ti)
            state[0, at] = a
            state[1, at] = q
            state[2, at] = tt
            state[3, at] = sb

    optics(7, 1)

    def up(i, _):
        grp = 7 - i
        optics(grp, 0)
        climb(grp, 1)
        optics(jnp.maximum(grp - 1, 0), 1)
        climb(grp, 0)
        return 0

    lax.fori_loop(0, 8, up, 0)

    def side(make):
        parts = [sum(make(c) for c in range(A_CHUNKS))]
        if tile.packed:
            parts.append(sum(make(c) for c in range(A_CHUNKS, chunks)))
        return jnp.concatenate(parts, axis=1)

    beams = [beam_top(c) for c in range(chunks)]
    surf = jnp.sum(side(lambda c: state[3, 8 * c:8 * c + 8] * beams[c]), axis=0, keepdims=True)
    slotted = row_times(surf, to_slot)
    if after_up is not None:
        after_up(slotted)

    net[0:8] = side(lambda c: beams[c] * (1.0 - state[1, 8 * c:8 * c + 8]))
    UNROLL = 4

    def down(i, carry):
        dn, bm = list(carry[0]), list(carry[1])
        for j in range(UNROLL):
            l = i * UNROLL + j
            total = [None, None]
            for c in range(chunks):
                w = pl.ds(pl.multiple_of(l * (8 * chunks) + 8 * c, 8), 8)
                d = coef[0, w] * dn[c] + coef[1, w] * bm[c]
                bb = bm[c] * coef[2, w]
                v = bb * coef[4, w] + d * coef[3, w]
                dn[c], bm[c] = d, bb
                which = 0 if c < A_CHUNKS else 1
                total[which] = v if total[which] is None else total[which] + v
            at = pl.ds(pl.multiple_of(l * 8 + 8, 8), 8)
            net[at, 0:WIDE] = total[0]
            if tile.packed:
                net[at, WIDE:] = total[1]
        return tuple(dn), tuple(bm)

    lax.fori_loop(0, NLEV // UNROLL, down, (tuple(jnp.zeros((8, WIDE), F32) for _ in range(chunks)), tuple(beams)))
    net[8 * 65:8 * 72] = jnp.zeros((56, lanes), F32)
    fl[...] = jnp.sum(net[...].reshape(72, 8, lanes), axis=1)
    hi, mid, low = thirds(fl[0:64] - fl[1:65])
    lost = dot(hi, spread) + dot(mid, spread) + dot(low, spread)
    heat = NLEV * lost / th[...]
    return heat, slotted


def scratch(tile):
    lanes, rows = tile.lanes, 8 * tile.chunks
    return [
        pltpu.VMEM((8, 1024, lanes), BF16),
        pltpu.VMEM((8, NG, 256), BF16),
        pltpu.VMEM((2, 4 * NG, 512), BF16),
        pltpu.VMEM((2, 3, 4 * NG, lanes), F32),
        pltpu.VMEM((4, rows, WIDE), F32),
        pltpu.VMEM((5, NLEV * rows, WIDE), F32),
        pltpu.VMEM((72 * 8, lanes), F32),
        pltpu.VMEM((72, lanes), F32),
        pltpu.VMEM((NG, lanes), F32),
    ]


def overflow_kernel(*refs):
    sun, hbm, (heat, slotted) = refs[0], refs[1:12], refs[12:14]
    local, sem, scr = refs[14:25], refs[25], refs[26:]
    heat[...] = jnp.zeros_like(heat)
    slotted[...] = jnp.zeros_like(slotted)

    @pl.when(jnp.sum(jnp.where(sun[...] == 1, 1, 0)) > MAIN)
    def _():
        for i in range(11):
            copy = pltpu.make_async_copy(hbm[i], local[i], sem.at[i])
            copy.start()
            copy.wait()
        ins = local[:7] + (sun,) + local[7:]
        h, s = physics(Tile(MAIN, False), ins, scr)
        heat[...] = h
        slotted[...] = s


def main_kernel(*refs):
    ins, (heat0, slotted0), (heat, surface) = refs[:12], refs[12:14], refs[14:16]
    send, recv, send_sem, recv_sem, go = refs[16:21]
    scr = refs[21:]
    e, c = lax.axis_index("elem"), lax.axis_index("col")
    me = e * N_COL + c

    barrier = pltpu.get_barrier_semaphore()
    for k in range(1, N_COL):
        pl.semaphore_signal(barrier, inc=1, device_id=(e, lax.rem(c + k, N_COL)), device_id_type=MESH)
    for k in range(1, N_ELEM):
        pl.semaphore_signal(barrier, inc=1, device_id=(lax.rem(e + k, N_ELEM), c), device_id_type=MESH)

    def ship(slotted):
        slotted = slotted + slotted0[...]
        at, s = iota((DEVS, CH), 0), iota((DEVS, CH), 1)
        own = jnp.where(s // 2 == at, slotted, 0.0)
        send[...] = (own[:, :128] + own[:, 128:]).reshape(DEVS, 1, 128)
        pl.semaphore_wait(barrier, N_COL - 1 + N_ELEM - 1)
        for k in range(1, N_ELEM):
            pl.semaphore_signal(go, inc=1, device_id=(lax.rem(e + k, N_ELEM), c), device_id_type=MESH)
        pl.semaphore_wait(go, N_ELEM - 1)
        recv[me] = send[me]

        def push(k, _):
            t = lax.rem(me + k, DEVS)
            pltpu.make_async_remote_copy(
                src_ref=send.at[t],
                dst_ref=recv.at[me],
                send_sem=send_sem,
                recv_sem=recv_sem,
                device_id=(t // N_COL, lax.rem(t, N_COL)),
                device_id_type=MESH,
            ).start()
            return 0

        lax.fori_loop(1, DEVS, push, 0)

    h, _ = physics(Tile(0, True), ins, scr, after_up=ship)
    heat[...] = h + heat0[...]
    rest = recv.at[pl.ds(0, DEVS - 1)]
    pltpu.make_async_copy(rest, rest, recv_sem).wait()
    pltpu.make_async_copy(rest, rest, send_sem).wait()
    got = recv[...].reshape(DEVS, 128)
    lane = iota((DEVS, 128), 1)
    first = lax.rem(2 * me, 128)
    even = jnp.sum(jnp.where(lane == first, got, 0.0), axis=1, keepdims=True)
    odd = jnp.sum(jnp.where(lane == first + 1, got, 0.0), axis=1, keepdims=True)
    at, s = iota((DEVS, CH), 0), iota((DEVS, CH), 1)
    surface[...] = jnp.sum(jnp.where(s // 2 == at, jnp.where(s % 2 == 0, even, odd), 0.0), axis=0, keepdims=True)


def body(*args):
    args = tuple(a.reshape(1, -1) if a.ndim == 1 else a for a in args)
    vmem, hbm = pl.BlockSpec(memory_space=pltpu.VMEM), pl.BlockSpec(memory_space=pl.ANY)
    outs = (jax.ShapeDtypeStruct((NLEV, CH), F32), jax.ShapeDtypeStruct((1, CH), F32))
    rest = args[:7] + args[8:]
    extra = pl.pallas_call(
        overflow_kernel,
        out_shape=outs,
        in_specs=[vmem] + [hbm] * 11,
        out_specs=(vmem, vmem),
        scratch_shapes=[pltpu.VMEM(a.shape, a.dtype) for a in rest] + [pltpu.SemaphoreType.DMA((11,))] + scratch(Tile(MAIN, False)),
        compiler_params=pltpu.CompilerParams(vmem_limit_bytes=60 * 2**20),
    )(args[7], *rest)
    heat, surface = pl.pallas_call(
        main_kernel,
        out_shape=outs,
        in_specs=[vmem] * 14,
        out_specs=(vmem, vmem),
        scratch_shapes=[
            pltpu.VMEM((DEVS, 1, 128), F32),
            pltpu.VMEM((DEVS, 1, 128), F32),
            pltpu.SemaphoreType.DMA,
            pltpu.SemaphoreType.DMA,
            pltpu.SemaphoreType.REGULAR,
        ]
        + scratch(Tile(0, True)),
        compiler_params=pltpu.CompilerParams(vmem_limit_bytes=60 * 2**20, collective_id=0, has_side_effects=True),
    )(*args, *extra)
    return heat, surface.reshape(CH)


def solution(mesh):
    columns = ("elem", "col")
    return jax.shard_map(
        body,
        mesh=mesh,
        in_specs=(
            P(None, None, columns),
            P(None, None, columns),
            P(None, None, columns),
            P(None, None, columns),
            P(None, columns),
            P(columns),
            P(None, columns),
            P(columns),
            P(columns, None),
            P(),
            P(),
            P(),
        ),
        out_specs=(P(None, columns), P(columns)),
        check_vma=False,
    )
```

```python
import functools
import math

import jax
import jax.numpy as jnp
from jax import lax
from jax.experimental import pallas as pl
from jax.experimental.pallas import tpu as pltpu
from jax.sharding import PartitionSpec as P

MESH = pl.DeviceIdType.MESH
F32 = jnp.float32
BF16 = jnp.bfloat16

NG = 112
NBND = 14
NSP = 8
NLEV = 64
CH = 256
N_ELEM = 8
N_COL = 16
DEVS = 128

WIDE = 128
NARROW = 32
MAIN = WIDE + NARROW
STARTS = (0, 32, 64, 88)
A_CHUNKS = NG // 8
B_CHUNKS = 4
SCALE = math.log2(math.e)


LIMIT = 56 * 2**20


def dot(a, b):
    return jnp.dot(a, b, preferred_element_type=F32)


def iota(shape, axis):
    return lax.broadcasted_iota(jnp.int32, shape, axis)


def one(mask):
    return jnp.where(mask, 1.0, 0.0).astype(BF16)


def halves(x):
    hi = x.astype(BF16)
    return hi, (x - hi.astype(F32)).astype(BF16)


def thirds(x):
    hi = x.astype(BF16)
    rest = x - hi.astype(F32)
    mid = rest.astype(BF16)
    return hi, mid, (rest - mid.astype(F32)).astype(BF16)


def row_times(row, matrix):
    hi, mid, low = thirds(row)
    at = iota((16, row.shape[1]), 0)
    stack = jnp.where(at == 0, hi.astype(F32), jnp.where(at == 1, mid.astype(F32), jnp.where(at == 2, low.astype(F32), 0.0)))
    return jnp.sum(dot(stack.astype(BF16), matrix), axis=0, keepdims=True)


class Tile:
    def __init__(self, first, packed):
        self.first = first
        self.packed = packed
        self.lanes = 2 * WIDE if packed else WIDE
        self.chunks = A_CHUNKS + (B_CHUNKS if packed else 0)

    def compact(self, lane):
        return self.first + jnp.where(lane < WIDE, lane, WIDE + lane % NARROW)


def physics(tile, refs, scr, loaded=None, midway=None, after_up=None):
    (ab, ct, cs, ca, th, mu, alb, sun, slot, kc, sol, band) = refs
    (rhs, masks, lhs, buf, state, coef, net, fl, albs) = scr
    lanes, chunks = tile.lanes, tile.chunks

    lit = jnp.where(sun[...] == 1, 1.0, 0.0)
    ri, ci = iota((CH, CH), 0), iota((CH, CH), 1)
    litb = jnp.broadcast_to(lit, (CH, CH))
    ones = jnp.ones((CH, CH), BF16)
    rank_c = dot(jnp.where(ci < ri, litb, 0.0).astype(BF16), ones[:, :lanes])
    lit_c = dot(jnp.where(ci == ri, litb, 0.0).astype(BF16), ones[:, :lanes])
    row_lit = jnp.broadcast_to(lit, (16, CH)).astype(BF16)
    rank_r = dot(row_lit, one(ri < ci))[0:1]
    count = dot(row_lit, ones)[0:1]
    want_c = tile.compact(iota((CH, lanes), 1)).astype(F32)
    gather = one(jnp.where(want_c >= count[:, :lanes], jnp.where(iota((CH, lanes), 0) == 0, 1.0, 0.0), jnp.where(rank_c == want_c, lit_c, 0.0)) > 0.5)
    want_r = tile.compact(iota((lanes, CH), 0)).astype(F32)
    spread = one(jnp.where(rank_r == want_r, jnp.broadcast_to(lit, (lanes, CH)), 0.0) > 0.5)
    to_slot = dot(spread, one(slot[...] == ri)).astype(BF16)

    eye = iota((NG, NG), 0) == iota((NG, NG), 1)
    solar = sol[...]
    weight = jnp.sum(jnp.where(eye, solar / jnp.sum(solar, axis=1, keepdims=True), 0.0), axis=1, keepdims=True)
    band_c = jnp.sum(jnp.where(eye, band[...].astype(F32), 0.0), axis=1, keepdims=True)
    k = iota((NG, CH), 1) % 128
    for l8 in range(8):
        pick = one((k // 8).astype(F32) == jnp.where(k % 8 == l8, band_c, -1.0))
        lhs[l8 // 4, (l8 % 4) * NG:(l8 % 4 + 1) * NG, 256:512] = pick
    for l8 in range(8):
        masks[l8] = one(iota((16, CH), 1) % 8 == l8)

    quarter = iota((8, WIDE), 1) // NARROW

    def pack(get, j):
        if j == 3:
            return jnp.where(quarter == 0, get(24), get(56))
        v = [get(s + 8 * j) for s in STARTS]
        return jnp.where(quarter == 0, v[0], jnp.where(quarter == 1, v[1], jnp.where(quarter == 2, v[2], v[3])))

    cosine = mu[...]
    cos = row_times(cosine, gather)
    cos_safe = jnp.where(cos > 0, cos, 1.0)
    rate = -1.0 / cos_safe
    wfull = jnp.broadcast_to(weight, (NG, WIDE))

    def lanes_of(x, c):
        return x[:, :WIDE] if c < A_CHUNKS else x[:, WIDE:]

    def chunk_of(c, get):
        if c < A_CHUNKS:
            return get(8 * c, 0)
        return pack(lambda row: get(row, WIDE), c - A_CHUNKS)

    def beam_top(c):
        w = chunk_of(c, lambda row, lane: wfull[row:row + 8])
        if c == A_CHUNKS + 3:
            w = jnp.where(quarter < 2, w, 0.0)
        return w * lanes_of(cos, c)

    def prepare(grp):
        rows = pl.ds(pl.multiple_of(grp * 8, 8), 8)
        thick = th[rows, :] * (SCALE / NLEV)
        gas = (ab[:, rows, :] * thick[None]).reshape(64, CH)
        tau = (ct[:, rows, :] * SCALE).reshape(112, CH)
        tau_s = tau * cs[:, rows, :].reshape(112, CH)
        tau_f = tau_s * ca[:, rows, :].reshape(112, CH)
        hi, low = halves(jnp.concatenate([gas, tau, tau_s, tau_f], axis=0))
        hi = dot(hi, gather).astype(BF16)
        low = dot(low, gather).astype(BF16)
        rhs[0:64] = hi[0:64]
        rhs[64:128] = low[0:64]
        rhs[128:192] = hi[0:64]
        rhs[192:256] = low[0:64]
        for i in range(3):
            at = 64 + 112 * i
            rhs[256 * i + 256:256 * i + 368] = hi[at:at + 112]
            rhs[256 * i + 384:256 * i + 496] = low[at:at + 112]
        k_rows = kc[:, rows, :].reshape(64, NG)
        k_hi = k_rows.astype(BF16).astype(F32)
        k_low = k_rows - k_hi
        k_t = jnp.concatenate(
            [jnp.concatenate([v, v], axis=0).T.astype(BF16) for v in (k_hi, k_low)], axis=1
        )
        for l8 in range(8):
            at = (l8 % 4) * NG
            lhs[l8 // 4, at:at + NG, 0:256] = k_t * jnp.concatenate([masks[l8]] * 7, axis=0)

    for i in range(3):
        rhs[256 * i + 368:256 * i + 384] = jnp.zeros((16, lanes), BF16)
        rhs[256 * i + 496:256 * i + 512] = jnp.zeros((16, lanes), BF16)

    def optics(hf):
        buf[hf, 0] = dot(lhs[hf], rhs[0:512])
        buf[hf, 1] = dot(lhs[hf, :, 256:512], rhs[512:768])
        buf[hf, 2] = dot(lhs[hf, :, 256:512], rhs[768:1024])

    def climb(grp, hf):
        for c in range(chunks):
            at = slice(8 * c, 8 * c + 8)
            a, q, tt, sb = (state[i, at] for i in range(4))
            m, r = lanes_of(cos_safe, c), lanes_of(rate, c)
            for j in (3, 2, 1, 0):
                t, s, f = (chunk_of(c, lambda row, lane: buf[hf, i, j * NG + row:j * NG + row + 8, lane:lane + WIDE]) for i in range(3))
                p1 = t - s
                p2 = t - f
                pp = p1 * p2
                kk = pp * lax.rsqrt(pp)
                nk2 = kk * -2.0
                e = jnp.exp2(nk2)
                e2 = e * e
                tot = p1 + p2
                inv_d = pl.reciprocal((tot - nk2) - e2 * (tot + nk2), approx=True)
                rdif = (s - f) * (1.0 - e2) * inv_d
                tdif = (kk * 4.0) * e * inv_d
                u = jnp.exp2(t * r)
                sc = (1.0 - u) * pl.reciprocal(t + t, approx=True)
                mf = m * f
                rdir = sc * (s - mf)
                tdir = sc * (s + mf)
                inv = pl.reciprocal(1.0 - rdif * a, approx=True)
                ti = tdif * inv
                qu = q * u
                b = (rdif * qu + tdir) * inv
                level = pl.multiple_of((grp * 8 + hf * 4 + j) * (8 * chunks), 8) + 8 * c
                w = pl.ds(pl.multiple_of(level, 8), 8)
                coef[0, w] = ti
                coef[1, w] = b
                coef[2, w] = u
                coef[3, w] = 1.0 - a
                coef[4, w] = 1.0 - q
                sb = tt * b + sb * u
                tt = tt * ti
                q = rdir + ti * (qu + a * tdir)
                a = rdif + tdif * (a * ti)
            state[0, at] = a
            state[1, at] = q
            state[2, at] = tt
            state[3, at] = sb

    if loaded is not None:
        loaded(0)
    a_hi, a_low = halves(jnp.concatenate([alb[...], jnp.zeros((2, CH), F32)], axis=0))
    zero = jnp.zeros((112, lanes), BF16)
    a_rhs = jnp.concatenate([dot(a_hi, gather).astype(BF16), zero, dot(a_low, gather).astype(BF16), zero], axis=0)
    albs[...] = dot(one(k.astype(F32) == band_c), a_rhs)
    for c in range(chunks):
        a = chunk_of(c, lambda row, lane: albs[row:row + 8, lane:lane + WIDE])
        at = slice(8 * c, 8 * c + 8)
        state[0, at] = a
        state[1, at] = a
        state[2, at] = jnp.ones((8, WIDE), F32)
        state[3, at] = jnp.ones((8, WIDE), F32)
    prepare(7)
    optics(1)
    if loaded is not None:
        loaded(1)

    def up(i, _):
        grp = 7 - i
        if midway is not None:
            pl.when(i == 5)(midway)
        optics(0)
        climb(grp, 1)
        prepare(jnp.maximum(grp - 1, 0))
        optics(1)
        climb(grp, 0)
        return 0

    lax.fori_loop(0, 8, up, 0)

    def side(make):
        parts = [sum(make(c) for c in range(A_CHUNKS))]
        if tile.packed:
            parts.append(sum(make(c) for c in range(A_CHUNKS, chunks)))
        return jnp.concatenate(parts, axis=1)

    beams = [beam_top(c) for c in range(chunks)]
    surf = jnp.sum(side(lambda c: state[3, 8 * c:8 * c + 8] * beams[c]), axis=0, keepdims=True)
    slotted = row_times(surf, to_slot)
    if after_up is not None:
        after_up(slotted)

    net[0:8] = side(lambda c: beams[c] * (1.0 - state[1, 8 * c:8 * c + 8]))
    UNROLL = 4

    def down(i, carry):
        dn, bm = list(carry[0]), list(carry[1])
        for j in range(UNROLL):
            l = i * UNROLL + j
            total = [None, None]
            for c in range(chunks):
                w = pl.ds(pl.multiple_of(l * (8 * chunks) + 8 * c, 8), 8)
                d = coef[0, w] * dn[c] + coef[1, w] * bm[c]
                bb = bm[c] * coef[2, w]
                v = bb * coef[4, w] + d * coef[3, w]
                dn[c], bm[c] = d, bb
                which = 0 if c < A_CHUNKS else 1
                total[which] = v if total[which] is None else total[which] + v
            at = pl.ds(pl.multiple_of(l * 8 + 8, 8), 8)
            net[at, 0:WIDE] = total[0]
            if tile.packed:
                net[at, WIDE:] = total[1]
        return tuple(dn), tuple(bm)

    lax.fori_loop(0, NLEV // UNROLL, down, (tuple(jnp.zeros((8, WIDE), F32) for _ in range(chunks)), tuple(beams)))
    net[8 * 65:8 * 72] = jnp.zeros((56, lanes), F32)
    fl[...] = jnp.sum(net[...].reshape(72, 8, lanes), axis=1)
    hi, mid, low = thirds(fl[0:64] - fl[1:65])
    lost = dot(hi, spread) + dot(mid, spread) + dot(low, spread)
    heat = NLEV * lost / th[...]
    return heat, slotted


def scratch(tile):
    lanes, rows = tile.lanes, 8 * tile.chunks
    return [
        pltpu.VMEM((1024, lanes), BF16),
        pltpu.VMEM((8, 16, 256), BF16),
        pltpu.VMEM((2, 4 * NG, 512), BF16),
        pltpu.VMEM((2, 3, 4 * NG, lanes), F32),
        pltpu.VMEM((4, rows, WIDE), F32),
        pltpu.VMEM((5, NLEV * rows, WIDE), F32),
        pltpu.VMEM((72 * 8, lanes), F32),
        pltpu.VMEM((72, lanes), F32),
        pltpu.VMEM((NG, lanes), F32),
    ]


def overflow_kernel(*refs):
    sun, hbm, outs = refs[0], refs[1:12], refs[12:14]
    local, vals, sem, scr = refs[14:25], refs[25:27], refs[27], refs[28:]

    @pl.when(jnp.sum(jnp.where(sun[...] == 1, 1.0, 0.0)) > MAIN)
    def _():
        for i in range(11):
            copy = pltpu.make_async_copy(hbm[i], local[i], sem.at[i])
            copy.start()
            copy.wait()
        ins = local[:7] + (sun,) + local[7:]
        h, s = physics(Tile(MAIN, False), ins, scr)
        vals[0][...] = h
        vals[1][...] = s
        for i in range(2):
            copy = pltpu.make_async_copy(vals[i], outs[i], sem.at[11 + i])
            copy.start()
            copy.wait()


def main_kernel(*refs):
    big, (mu, alb_hbm, sun, slot, kc_hbm, sol, band) = refs[:5], refs[5:12]
    heat0_hbm, slotted0, (heat, surface) = refs[12], refs[13], refs[14:16]
    send, recv, heat0, send_sem, recv_sem, go, in_sem = refs[16:23]
    local, alb, kc, scr = refs[23:28], refs[28], refs[29], refs[30:]
    small = (mu, alb, sun, slot, kc, sol, band)
    e, c = lax.axis_index("elem"), lax.axis_index("col")
    me = e * N_COL + c

    def pieces(first):
        got = []
        for i in range(5):
            rows = pl.ds(NLEV - 8, 8) if first else pl.ds(0, NLEV - 8)
            src, dst = (r.at[rows] if i == 4 else r.at[:, rows] for r in (big[i], local[i]))
            got.append(pltpu.make_async_copy(src, dst, in_sem.at[i if first else 5 + i]))
        if first:
            got.append(pltpu.make_async_copy(alb_hbm, alb, in_sem.at[11]))
            got.append(pltpu.make_async_copy(kc_hbm, kc, in_sem.at[12]))
        else:
            got.append(pltpu.make_async_copy(heat0_hbm, heat0, in_sem.at[10]))
        return got

    for first in (True, False):
        for copy in pieces(first):
            copy.start()

    barrier = pltpu.get_barrier_semaphore()
    for k in range(1, N_COL):
        pl.semaphore_signal(barrier, inc=1, device_id=(e, lax.rem(c + k, N_COL)), device_id_type=MESH)
    for k in range(1, N_ELEM):
        pl.semaphore_signal(barrier, inc=1, device_id=(lax.rem(e + k, N_ELEM), c), device_id_type=MESH)

    def loaded(part):
        for copy in pieces(part == 0):
            copy.wait()

    def midway():
        pl.semaphore_wait(barrier, N_COL - 1 + N_ELEM - 1)
        for k in range(1, N_ELEM):
            pl.semaphore_signal(go, inc=1, device_id=(lax.rem(e + k, N_ELEM), c), device_id_type=MESH)

    many = jnp.sum(jnp.where(sun[...] == 1, 1.0, 0.0), axis=1, keepdims=True) > MAIN

    def ship(slotted):
        slotted = slotted + jnp.where(many, slotted0[...], 0.0)
        at, s = iota((DEVS, CH), 0), iota((DEVS, CH), 1)
        own = jnp.where(s // 2 == at, slotted, 0.0)
        send[...] = (own[:, :128] + own[:, 128:]).reshape(DEVS, 1, 128)
        pl.semaphore_wait(go, N_ELEM - 1)
        for te, tc in farthest_first(e, c):
            pltpu.make_async_remote_copy(
                src_ref=send.at[te * N_COL + tc],
                dst_ref=recv.at[me],
                send_sem=send_sem,
                recv_sem=recv_sem,
                device_id=(te, tc),
                device_id_type=MESH,
            ).start()
        recv[me] = send[me]

    h, _ = physics(Tile(0, True), local + small, scr, loaded=loaded, midway=midway, after_up=ship)
    heat[...] = h + jnp.where(many, heat0[...], 0.0)
    rest = recv.at[pl.ds(0, DEVS - 1)]
    pltpu.make_async_copy(rest, rest, recv_sem).wait()
    got = recv[...].reshape(DEVS, 128)
    lane = iota((DEVS, 128), 1)
    first = lax.rem(2 * me, 128)
    even = jnp.sum(jnp.where(lane == first, got, 0.0), axis=1, keepdims=True)
    odd = jnp.sum(jnp.where(lane == first + 1, got, 0.0), axis=1, keepdims=True)
    at, s = iota((DEVS, CH), 0), iota((DEVS, CH), 1)
    surface[...] = jnp.sum(jnp.where(s // 2 == at, jnp.where(s % 2 == 0, even, odd), 0.0), axis=0, keepdims=True)
    pltpu.make_async_copy(rest, rest, send_sem).wait()


def farthest_first(e, c):
    y, core, x, z = e // 2, lax.rem(e, 2), c // 4, lax.rem(c, 4)
    ys = [lax.rem(y + i, 4) * 2 for i in range(4)]
    cores = [core, 1 - core]
    xs = [lax.rem(x + i, 4) * 4 for i in range(4)]
    zs = [lax.rem(z + i, 4) for i in range(4)]
    elems = {(i, j): ys[i] + cores[j] for i in range(4) for j in range(2)}
    cols = {(i, j): xs[i] + zs[j] for i in range(4) for j in range(4)}
    hops = (0, 1, 2, 1)
    steps = [(i, j, k, m) for i in range(4) for j in range(2) for k in range(4) for m in range(4)][1:]
    steps.sort(key=lambda d: (-(hops[d[0]] + hops[d[2]] + hops[d[3]]), -d[1]))
    return [(elems[d[0], d[1]], cols[d[2], d[3]]) for d in steps]


def body(*args):
    args = tuple(a.reshape(1, -1) if a.ndim == 1 else a for a in args)
    vmem, hbm = pl.BlockSpec(memory_space=pltpu.VMEM), pl.BlockSpec(memory_space=pltpu.HBM)
    outs = (jax.ShapeDtypeStruct((NLEV, CH), F32), jax.ShapeDtypeStruct((1, CH), F32))
    rest = args[:7] + args[8:]
    extra = pl.pallas_call(
        overflow_kernel,
        out_shape=outs,
        in_specs=[vmem] + [hbm] * 11,
        out_specs=(hbm, hbm),
        scratch_shapes=[pltpu.VMEM(a.shape, a.dtype) for a in rest]
        + [pltpu.VMEM((NLEV, CH), F32), pltpu.VMEM((1, CH), F32), pltpu.SemaphoreType.DMA((13,))]
        + scratch(Tile(MAIN, False)),
        compiler_params=pltpu.CompilerParams(vmem_limit_bytes=LIMIT),
    )(args[7], *rest)
    heat, surface = pl.pallas_call(
        main_kernel,
        out_shape=(pltpu.VMEM((NLEV, CH), F32), pltpu.VMEM((1, CH), F32)),
        in_specs=[hbm] * 5 + [vmem, hbm, vmem, vmem, hbm, vmem, vmem] + [hbm, vmem],
        out_specs=(vmem, vmem),
        scratch_shapes=[
            pltpu.VMEM((DEVS, 1, 128), F32),
            pltpu.VMEM((DEVS, 1, 128), F32),
            pltpu.VMEM((NLEV, CH), F32),
            pltpu.SemaphoreType.DMA,
            pltpu.SemaphoreType.DMA,
            pltpu.SemaphoreType.REGULAR,
            pltpu.SemaphoreType.DMA((13,)),
        ]
        + [pltpu.VMEM(a.shape, a.dtype) for a in args[:5] + (args[6], args[9])]
        + scratch(Tile(0, True)),
        compiler_params=pltpu.CompilerParams(vmem_limit_bytes=LIMIT, collective_id=0, has_side_effects=True),
    )(*args, *extra)
    return heat, surface.reshape(CH)


def solution(mesh):
    columns = ("elem", "col")
    return jax.shard_map(
        body,
        mesh=mesh,
        in_specs=(
            P(None, None, columns),
            P(None, None, columns),
            P(None, None, columns),
            P(None, None, columns),
            P(None, columns),
            P(columns),
            P(None, columns),
            P(columns),
            P(columns, None),
            P(),
            P(),
            P(),
        ),
        out_specs=(P(None, columns), P(columns)),
        check_vma=False,
    )
```

```python
import functools
import math

import jax
import jax.numpy as jnp
from jax import lax
from jax.experimental import pallas as pl
from jax.experimental.pallas import tpu as pltpu
from jax.sharding import PartitionSpec as P

MESH = pl.DeviceIdType.MESH
F32 = jnp.float32
BF16 = jnp.bfloat16

NG = 112
NBND = 14
NSP = 8
NLEV = 64
CH = 256
N_ELEM = 8
N_COL = 16
DEVS = 128

WIDE = 128
NARROW = 32
MAIN = WIDE + NARROW
STARTS = (0, 32, 64, 88)
A_CHUNKS = NG // 8
B_CHUNKS = 4
SCALE = math.log2(math.e)


LIMIT = 56 * 2**20


def dot(a, b):
    return jnp.dot(a, b, preferred_element_type=F32)


def iota(shape, axis):
    return lax.broadcasted_iota(jnp.int32, shape, axis)


def one(mask):
    return jnp.where(mask, 1.0, 0.0).astype(BF16)


def halves(x):
    hi = x.astype(BF16)
    return hi, (x - hi.astype(F32)).astype(BF16)


def thirds(x):
    hi = x.astype(BF16)
    rest = x - hi.astype(F32)
    mid = rest.astype(BF16)
    return hi, mid, (rest - mid.astype(F32)).astype(BF16)


def row_times(row, matrix):
    hi, mid, low = thirds(row)
    at = iota((16, row.shape[1]), 0)
    stack = jnp.where(at == 0, hi.astype(F32), jnp.where(at == 1, mid.astype(F32), jnp.where(at == 2, low.astype(F32), 0.0)))
    return jnp.sum(dot(stack.astype(BF16), matrix), axis=0, keepdims=True)


class Tile:
    def __init__(self, first, packed):
        self.first = first
        self.packed = packed
        self.lanes = 2 * WIDE if packed else WIDE
        self.chunks = A_CHUNKS + (B_CHUNKS if packed else 0)

    def compact(self, lane):
        return self.first + jnp.where(lane < WIDE, lane, WIDE + lane % NARROW)


def physics(tile, refs, scr, loaded=None, midway=None, after_down=None):
    (ab, ct, cs, ca, th, mu, alb, sun, slot, kc, sol, band) = refs
    (rhs, taus, masks, mixed, lhs, buf, state, coef, net, fl, albs) = scr
    lanes, chunks = tile.lanes, tile.chunks

    lit = jnp.where(sun[...] == 1, 1.0, 0.0)
    ri, ci = iota((CH, CH), 0), iota((CH, CH), 1)
    litb = jnp.broadcast_to(lit, (CH, CH))
    ones = jnp.ones((CH, CH), BF16)
    rank_c = dot(jnp.where(ci < ri, litb, 0.0).astype(BF16), ones[:, :lanes])
    lit_c = dot(jnp.where(ci == ri, litb, 0.0).astype(BF16), ones[:, :lanes])
    row_lit = jnp.broadcast_to(lit, (16, CH)).astype(BF16)
    rank_r = dot(row_lit, one(ri < ci))[0:1]
    count = dot(row_lit, ones)[0:1]
    want_c = tile.compact(iota((CH, lanes), 1)).astype(F32)
    gather = one(jnp.where(want_c >= count[:, :lanes], jnp.where(iota((CH, lanes), 0) == 0, 1.0, 0.0), jnp.where(rank_c == want_c, lit_c, 0.0)) > 0.5)
    want_r = tile.compact(iota((lanes, CH), 0)).astype(F32)
    spread = one(jnp.where(rank_r == want_r, jnp.broadcast_to(lit, (lanes, CH)), 0.0) > 0.5)
    to_slot = dot(spread, one(slot[...] == ri)).astype(BF16)

    eye = iota((NG, NG), 0) == iota((NG, NG), 1)
    solar = sol[...]
    weight = jnp.sum(jnp.where(eye, solar / jnp.sum(solar, axis=1, keepdims=True), 0.0), axis=1, keepdims=True)
    band_c = jnp.sum(jnp.where(eye, band[...].astype(F32), 0.0), axis=1, keepdims=True)
    k = iota((NG, CH), 1) % 128
    for l8 in range(8):
        pick = one((k // 8).astype(F32) == jnp.where(k % 8 == l8, band_c, -1.0))
        lhs[l8 // 4, (l8 % 4) * NG:(l8 % 4 + 1) * NG, 256:512] = pick
    k4 = iota((NG, CH), 1) - 96
    k4 = jnp.where(k4 >= 56, k4 - 56, k4)
    b4 = jnp.where(iota((NG, CH), 1) < 96, -2.0, (k4 // 4).astype(F32))
    for j in range(4):
        masks[j] = one(iota((16, 128), 1) % 4 == j)
        pick = one(b4 == jnp.where(k4 % 4 == j, band_c, -1.0))
        mixed[j] = pick[:, 0:128]
        for hf in range(2):
            lhs[hf, j * NG:(j + 1) * NG, 128:256] = pick[:, 128:256]

    quarter = iota((8, WIDE), 1) // NARROW

    def pack(get, j):
        if j == 3:
            return jnp.where(quarter == 0, get(24), get(56))
        v = [get(s + 8 * j) for s in STARTS]
        return jnp.where(quarter == 0, v[0], jnp.where(quarter == 1, v[1], jnp.where(quarter == 2, v[2], v[3])))

    cosine = mu[...]
    cos = row_times(cosine, gather)
    cos_safe = jnp.where(cos > 0, cos, 1.0)
    rate = -1.0 / cos_safe
    wfull = jnp.broadcast_to(weight, (NG, WIDE))

    def lanes_of(x, c):
        return x[:, :WIDE] if c < A_CHUNKS else x[:, WIDE:]

    def chunk_of(c, get):
        if c < A_CHUNKS:
            return get(8 * c, 0)
        return pack(lambda row: get(row, WIDE), c - A_CHUNKS)

    def beam_top(c):
        w = chunk_of(c, lambda row, lane: wfull[row:row + 8])
        if c == A_CHUNKS + 3:
            w = jnp.where(quarter < 2, w, 0.0)
        return w * lanes_of(cos, c) * 0.5

    def prepare(grp):
        rows = pl.ds(pl.multiple_of(grp * 8, 8), 8)
        thick = th[rows, :] * (SCALE / NLEV)
        gas = (ab[:, rows, :] * thick[None]).reshape(64, CH)
        tau = (ct[:, rows, :] * SCALE).reshape(112, CH)
        tau_s = tau * cs[:, rows, :].reshape(112, CH)
        tau_f = tau_s * ca[:, rows, :].reshape(112, CH)
        hi, low = halves(jnp.concatenate([gas, tau, tau_s, tau_f], axis=0))
        hi = dot(hi, gather)
        low = dot(low, gather)
        hi_f, low_f = hi, low
        for i in range(2):
            at = 176 + 112 * i
            rhs[256 * i:256 * i + 112] = hi_f[at:at + 112].astype(BF16)
            rhs[256 * i + 128:256 * i + 240] = low_f[at:at + 112].astype(BF16)
        k_rows = kc[:, rows, :].reshape(64, NG)
        k_hi = k_rows.astype(BF16).astype(F32)
        k_low = k_rows - k_hi

        def four(x, count, hf):
            return jnp.concatenate([x[8 * i + 4 * hf:8 * i + 4 * hf + 4] for i in range(count)], axis=0)

        for hf in range(2):
            g_hi, g_low = four(hi_f, 8, hf), four(low_f, 8, hf)
            c_hi, c_low = four(hi_f[64:176], 14, hf), four(low_f[64:176], 14, hf)
            taus[hf] = jnp.concatenate([g_hi, g_low, g_hi, c_hi, c_low, jnp.zeros((48, lanes), F32)], axis=0).astype(BF16)
            kh, kl = four(k_hi, 8, hf), four(k_low, 8, hf)
            k_t = jnp.concatenate([kh, kh, kl, jnp.zeros((32, NG), F32)], axis=0).T.astype(BF16)
            for j in range(4):
                at = j * NG
                lhs[hf, at:at + NG, 0:128] = k_t * jnp.concatenate([masks[j]] * 7, axis=0) + mixed[j]

    for i in range(2):
        rhs[256 * i + 112:256 * i + 128] = jnp.zeros((16, lanes), BF16)
        rhs[256 * i + 240:256 * i + 256] = jnp.zeros((16, lanes), BF16)

    def optics(hf):
        buf[hf, 0] = dot(lhs[hf, :, 0:256], taus[hf])
        buf[hf, 1] = dot(lhs[hf, :, 256:512], rhs[0:256])
        buf[hf, 2] = dot(lhs[hf, :, 256:512], rhs[256:512])

    def descend(grp, hf):
        for c in range(chunks):
            at = slice(8 * c, 8 * c + 8)
            refl, diff, beam = (state[i, at] for i in range(3))
            m, r = lanes_of(cos_safe, c), lanes_of(rate, c)
            for j in range(4):
                t, s, f = (chunk_of(c, lambda row, lane: buf[hf, i, j * NG + row:j * NG + row + 8, lane:lane + WIDE]) for i in range(3))
                p1 = t - s
                p2 = t - f
                pp = p1 * p2
                kk = pp * lax.rsqrt(pp)
                nk2 = kk * -2.0
                e = jnp.exp2(nk2)
                e2 = e * e
                tot = p1 + p2
                inv_d = pl.reciprocal((tot - nk2) - e2 * (tot + nk2), approx=True)
                rdif = (s - f) * (1.0 - e2) * inv_d
                tdif = (kk * 4.0) * e * inv_d
                below = beam * jnp.exp2(t * r)
                sc = (beam - below) * pl.reciprocal(t, approx=True)
                mf = m * f
                s_up = sc * (s - mf)
                s_dn = sc * (s + mf)
                inv = pl.reciprocal(1.0 - rdif * refl, approx=True)
                ti = tdif * inv
                level = pl.multiple_of((grp * 8 + hf * 4 + j) * (8 * chunks), 8) + 8 * c
                w = pl.ds(pl.multiple_of(level, 8), 8)
                coef[0, w] = ti
                coef[1, w] = refl
                coef[2, w] = diff
                coef[3, w] = s_up
                coef[4, w] = rdif * inv
                coef[5, w] = beam
                diff = s_dn + ti * (diff + refl * s_up)
                refl = rdif + tdif * (refl * ti)
                beam = below
            state[0, at] = refl
            state[1, at] = diff
            state[2, at] = beam

    if loaded is not None:
        loaded(0)
    a_hi, a_low = halves(jnp.concatenate([alb[...], jnp.zeros((2, CH), F32)], axis=0))
    zero = jnp.zeros((112, lanes), BF16)
    a_rhs = jnp.concatenate([dot(a_hi, gather).astype(BF16), zero, dot(a_low, gather).astype(BF16), zero], axis=0)
    albs[...] = dot(one(k.astype(F32) == band_c), a_rhs)
    for c in range(chunks):
        at = slice(8 * c, 8 * c + 8)
        state[0, at] = jnp.zeros((8, WIDE), F32)
        state[1, at] = jnp.zeros((8, WIDE), F32)
        state[2, at] = beam_top(c)
    prepare(0)
    optics(0)
    if loaded is not None:
        loaded(1)

    def downward(i, _):
        grp = i
        if midway is not None:
            pl.when(i == 5)(midway)
        optics(1)
        descend(grp, 0)
        prepare(jnp.minimum(grp + 1, 7))
        optics(0)
        descend(grp, 1)
        return 0

    lax.fori_loop(0, 8, downward, 0)

    def side(make):
        parts = [sum(make(c) for c in range(A_CHUNKS))]
        if tile.packed:
            parts.append(sum(make(c) for c in range(A_CHUNKS, chunks)))
        return jnp.concatenate(parts, axis=1)

    flux, ups = [], []
    for c in range(chunks):
        refl, diff, beam = (state[i, 8 * c:8 * c + 8] for i in range(3))
        al = chunk_of(c, lambda row, lane: albs[row:row + 8, lane:lane + WIDE])
        beam = beam + beam
        back = refl * al
        flux.append(beam + (diff + back * beam) * pl.reciprocal(1.0 - back, approx=True))
        ups.append(al * flux[-1])
    surf = jnp.sum(side(lambda c: flux[c]), axis=0, keepdims=True)
    slotted = row_times(surf, to_slot)
    if after_down is not None:
        after_down(slotted)

    net[8 * NLEV:8 * NLEV + 8] = side(lambda c: flux[c] - ups[c])
    UNROLL = 4

    def rise(i, carry):
        up_flux = list(carry)
        for j in range(UNROLL):
            l = NLEV - 1 - (i * UNROLL + j)
            total = [None, None]
            for c in range(chunks):
                w = pl.ds(pl.multiple_of(l * (8 * chunks) + 8 * c, 8), 8)
                ti, refl, diff, s_up, ri, beam = (coef[k, w] for k in range(6))
                up_flux[c] = ti * up_flux[c] + (ri * (diff + refl * s_up) + s_up)
                v = (beam + beam) + ((diff + refl * up_flux[c]) - up_flux[c])
                which = 0 if c < A_CHUNKS else 1
                total[which] = v if total[which] is None else total[which] + v
            at = pl.ds(pl.multiple_of(l * 8, 8), 8)
            net[at, 0:WIDE] = total[0]
            if tile.packed:
                net[at, WIDE:] = total[1]
        return tuple(up_flux)

    lax.fori_loop(0, NLEV // UNROLL, rise, tuple(ups))
    net[8 * 65:8 * 72] = jnp.zeros((56, lanes), F32)
    fl[...] = jnp.sum(net[...].reshape(72, 8, lanes), axis=1)
    hi, mid, low = thirds(fl[0:64] - fl[1:65])
    lost = dot(hi, spread) + dot(mid, spread) + dot(low, spread)
    heat = NLEV * lost / th[...]
    return heat, slotted


def scratch(tile):
    lanes, rows = tile.lanes, 8 * tile.chunks
    return [
        pltpu.VMEM((512, lanes), BF16),
        pltpu.VMEM((2, 256, lanes), BF16),
        pltpu.VMEM((4, 16, 128), BF16),
        pltpu.VMEM((4, NG, 128), BF16),
        pltpu.VMEM((2, 4 * NG, 512), BF16),
        pltpu.VMEM((2, 3, 4 * NG, lanes), F32),
        pltpu.VMEM((3, rows, WIDE), F32),
        pltpu.VMEM((6, NLEV * rows, WIDE), F32),
        pltpu.VMEM((72 * 8, lanes), F32),
        pltpu.VMEM((72, lanes), F32),
        pltpu.VMEM((NG, lanes), F32),
    ]


def overflow_kernel(*refs):
    sun, hbm, outs = refs[0], refs[1:12], refs[12:14]
    local, vals, sem, scr = refs[14:25], refs[25:27], refs[27], refs[28:]

    @pl.when(jnp.sum(jnp.where(sun[...] == 1, 1.0, 0.0)) > MAIN)
    def _():
        for i in range(11):
            copy = pltpu.make_async_copy(hbm[i], local[i], sem.at[i])
            copy.start()
            copy.wait()
        ins = local[:7] + (sun,) + local[7:]
        h, s = physics(Tile(MAIN, False), ins, scr)
        vals[0][...] = h
        vals[1][...] = s
        for i in range(2):
            copy = pltpu.make_async_copy(vals[i], outs[i], sem.at[11 + i])
            copy.start()
            copy.wait()


def main_kernel(*refs):
    big, (mu, alb_hbm, sun, slot, kc_hbm, sol, band) = refs[:5], refs[5:12]
    heat0_hbm, slotted0, (heat, surface) = refs[12], refs[13], refs[14:16]
    send, recv, heat0, send_sem, recv_sem, go, in_sem = refs[16:23]
    local, alb, kc, scr = refs[23:28], refs[28], refs[29], refs[30:]
    small = (mu, alb, sun, slot, kc, sol, band)
    e, c = lax.axis_index("elem"), lax.axis_index("col")
    me = e * N_COL + c

    def pieces(first):
        got = []
        for i in range(5):
            rows = pl.ds(0, 8) if first else pl.ds(8, NLEV - 8)
            src, dst = (r.at[rows] if i == 4 else r.at[:, rows] for r in (big[i], local[i]))
            got.append(pltpu.make_async_copy(src, dst, in_sem.at[i if first else 5 + i]))
        if first:
            got.append(pltpu.make_async_copy(alb_hbm, alb, in_sem.at[11]))
            got.append(pltpu.make_async_copy(kc_hbm, kc, in_sem.at[12]))
        else:
            got.append(pltpu.make_async_copy(heat0_hbm, heat0, in_sem.at[10]))
        return got

    for first in (True, False):
        for copy in pieces(first):
            copy.start()

    barrier = pltpu.get_barrier_semaphore()
    for k in range(1, N_COL):
        pl.semaphore_signal(barrier, inc=1, device_id=(e, lax.rem(c + k, N_COL)), device_id_type=MESH)
    for k in range(1, N_ELEM):
        pl.semaphore_signal(barrier, inc=1, device_id=(lax.rem(e + k, N_ELEM), c), device_id_type=MESH)

    def loaded(part):
        for copy in pieces(part == 0):
            copy.wait()

    def midway():
        pl.semaphore_wait(barrier, N_COL - 1 + N_ELEM - 1)
        for k in range(1, N_ELEM):
            pl.semaphore_signal(go, inc=1, device_id=(lax.rem(e + k, N_ELEM), c), device_id_type=MESH)

    many = jnp.sum(jnp.where(sun[...] == 1, 1.0, 0.0), axis=1, keepdims=True) > MAIN

    def ship(slotted):
        slotted = slotted + jnp.where(many, slotted0[...], 0.0)
        at, s = iota((DEVS, CH), 0), iota((DEVS, CH), 1)
        own = jnp.where(s // 2 == at, slotted, 0.0)
        send[...] = (own[:, :128] + own[:, 128:]).reshape(DEVS, 1, 128)
        pl.semaphore_wait(go, N_ELEM - 1)
        for te, tc in farthest_first(e, c):
            pltpu.make_async_remote_copy(
                src_ref=send.at[te * N_COL + tc],
                dst_ref=recv.at[me],
                send_sem=send_sem,
                recv_sem=recv_sem,
                device_id=(te, tc),
                device_id_type=MESH,
            ).start()
        recv[me] = send[me]

    h, _ = physics(Tile(0, True), local + small, scr, loaded=loaded, midway=midway, after_down=ship)
    heat[...] = h + jnp.where(many, heat0[...], 0.0)
    rest = recv.at[pl.ds(0, DEVS - 1)]
    pltpu.make_async_copy(rest, rest, recv_sem).wait()
    got = recv[...].reshape(DEVS, 128)
    lane = iota((DEVS, 128), 1)
    first = lax.rem(2 * me, 128)
    even = jnp.sum(jnp.where(lane == first, got, 0.0), axis=1, keepdims=True)
    odd = jnp.sum(jnp.where(lane == first + 1, got, 0.0), axis=1, keepdims=True)
    at, s = iota((DEVS, CH), 0), iota((DEVS, CH), 1)
    surface[...] = jnp.sum(jnp.where(s // 2 == at, jnp.where(s % 2 == 0, even, odd), 0.0), axis=0, keepdims=True)
    pltpu.make_async_copy(rest, rest, send_sem).wait()


def store_kernel(heat, surface, heat_out, surface_out, sem):
    copies = [pltpu.make_async_copy(heat, heat_out, sem.at[0]), pltpu.make_async_copy(surface, surface_out, sem.at[1])]
    for copy in copies:
        copy.start()
    for copy in copies:
        copy.wait()


def farthest_first(e, c):
    y, core, x, z = e // 2, lax.rem(e, 2), c // 4, lax.rem(c, 4)
    ys = [lax.rem(y + i, 4) * 2 for i in range(4)]
    cores = [core, 1 - core]
    xs = [lax.rem(x + i, 4) * 4 for i in range(4)]
    zs = [lax.rem(z + i, 4) for i in range(4)]
    elems = {(i, j): ys[i] + cores[j] for i in range(4) for j in range(2)}
    cols = {(i, j): xs[i] + zs[j] for i in range(4) for j in range(4)}
    hops = (0, 1, 2, 1)
    steps = [(i, j, k, m) for i in range(4) for j in range(2) for k in range(4) for m in range(4)][1:]
    steps.sort(key=lambda d: (-(hops[d[0]] + hops[d[2]] + hops[d[3]]), -d[1]))
    return [(elems[d[0], d[1]], cols[d[2], d[3]]) for d in steps]


def body(*args):
    args = tuple(a.reshape(1, -1) if a.ndim == 1 else a for a in args)
    vmem, hbm = pl.BlockSpec(memory_space=pltpu.VMEM), pl.BlockSpec(memory_space=pltpu.HBM)
    outs = (jax.ShapeDtypeStruct((NLEV, CH), F32), jax.ShapeDtypeStruct((1, CH), F32))
    rest = args[:7] + args[8:]
    extra = pl.pallas_call(
        overflow_kernel,
        out_shape=outs,
        in_specs=[vmem] + [hbm] * 11,
        out_specs=(hbm, hbm),
        scratch_shapes=[pltpu.VMEM(a.shape, a.dtype) for a in rest]
        + [pltpu.VMEM((NLEV, CH), F32), pltpu.VMEM((1, CH), F32), pltpu.SemaphoreType.DMA((13,))]
        + scratch(Tile(MAIN, False)),
        compiler_params=pltpu.CompilerParams(vmem_limit_bytes=LIMIT),
    )(args[7], *rest)
    heat, surface = pl.pallas_call(
        main_kernel,
        out_shape=(pltpu.VMEM((NLEV, CH), F32), pltpu.VMEM((1, CH), F32)),
        in_specs=[hbm] * 5 + [vmem, hbm, vmem, vmem, hbm, vmem, vmem] + [hbm, vmem],
        out_specs=(vmem, vmem),
        scratch_shapes=[
            pltpu.VMEM((DEVS, 1, 128), F32),
            pltpu.VMEM((DEVS, 1, 128), F32),
            pltpu.VMEM((NLEV, CH), F32),
            pltpu.SemaphoreType.DMA,
            pltpu.SemaphoreType.DMA,
            pltpu.SemaphoreType.REGULAR,
            pltpu.SemaphoreType.DMA((13,)),
        ]
        + [pltpu.VMEM(a.shape, a.dtype) for a in args[:5] + (args[6], args[9])]
        + scratch(Tile(0, True)),
        compiler_params=pltpu.CompilerParams(vmem_limit_bytes=LIMIT, collective_id=0, has_side_effects=True),
    )(*args, *extra)
    heat, surface = pl.pallas_call(
        store_kernel,
        out_shape=outs,
        in_specs=[vmem, vmem],
        out_specs=(hbm, hbm),
        scratch_shapes=[pltpu.SemaphoreType.DMA((2,))],
        compiler_params=pltpu.CompilerParams(vmem_limit_bytes=2 * 2**20),
    )(heat, surface)
    return heat, surface.reshape(CH)


def solution(mesh):
    columns = ("elem", "col")
    return jax.shard_map(
        body,
        mesh=mesh,
        in_specs=(
            P(None, None, columns),
            P(None, None, columns),
            P(None, None, columns),
            P(None, None, columns),
            P(None, columns),
            P(columns),
            P(None, columns),
            P(columns),
            P(columns, None),
            P(),
            P(),
            P(),
        ),
        out_specs=(P(None, columns), P(columns)),
        check_vma=False,
    )
```

```python
import functools
import math

import jax
import jax.numpy as jnp
from jax import lax
from jax.experimental import pallas as pl
from jax.experimental.pallas import tpu as pltpu
from jax.sharding import PartitionSpec as P

MESH = pl.DeviceIdType.MESH
F32 = jnp.float32
BF16 = jnp.bfloat16

NG = 112
NBND = 14
NSP = 8
NLEV = 64
CH = 256
N_ELEM = 8
N_COL = 16
DEVS = 128

WIDE = 128
NARROW = 32
MAIN = WIDE + NARROW
STARTS = (0, 32, 64, 88)
A_CHUNKS = NG // 8
B_CHUNKS = 4
SCALE = math.log2(math.e)


LIMIT = 56 * 2**20


def dot(a, b):
    return jnp.dot(a, b, preferred_element_type=F32)


def iota(shape, axis):
    return lax.broadcasted_iota(jnp.int32, shape, axis)


def one(mask):
    return jnp.where(mask, 1.0, 0.0).astype(BF16)


def halves(x):
    hi = x.astype(BF16)
    return hi, (x - hi.astype(F32)).astype(BF16)


def thirds(x):
    hi = x.astype(BF16)
    rest = x - hi.astype(F32)
    mid = rest.astype(BF16)
    return hi, mid, (rest - mid.astype(F32)).astype(BF16)


def row_times(row, matrix):
    hi, mid, low = thirds(row)
    at = iota((16, row.shape[1]), 0)
    stack = jnp.where(at == 0, hi.astype(F32), jnp.where(at == 1, mid.astype(F32), jnp.where(at == 2, low.astype(F32), 0.0)))
    return jnp.sum(dot(stack.astype(BF16), matrix), axis=0, keepdims=True)


class Tile:
    def __init__(self, first, packed):
        self.first = first
        self.packed = packed
        self.lanes = 2 * WIDE if packed else WIDE
        self.chunks = A_CHUNKS + (B_CHUNKS if packed else 0)

    def compact(self, lane):
        return self.first + jnp.where(lane < WIDE, lane, WIDE + lane % NARROW)


def physics(tile, refs, scr, loaded=None, midway=None, after_down=None):
    (ab, ct, cs, ca, th, mu, alb, sun, slot, kc, sol, band) = refs
    (rhs, taus, masks, mixed, lhs, buf, state, coef, net, fl, albs) = scr
    lanes, chunks = tile.lanes, tile.chunks

    lit = jnp.where(sun[...] == 1, 1.0, 0.0)
    ri, ci = iota((CH, CH), 0), iota((CH, CH), 1)
    litb = jnp.broadcast_to(lit, (CH, CH))
    ones = jnp.ones((CH, CH), BF16)
    rank_c = dot(jnp.where(ci < ri, litb, 0.0).astype(BF16), ones[:, :lanes])
    lit_c = dot(jnp.where(ci == ri, litb, 0.0).astype(BF16), ones[:, :lanes])
    row_lit = jnp.broadcast_to(lit, (16, CH)).astype(BF16)
    rank_r = dot(row_lit, one(ri < ci))[0:1]
    count = dot(row_lit, ones)[0:1]
    want_c = tile.compact(iota((CH, lanes), 1)).astype(F32)
    gather = one(jnp.where(want_c >= count[:, :lanes], jnp.where(iota((CH, lanes), 0) == 0, 1.0, 0.0), jnp.where(rank_c == want_c, lit_c, 0.0)) > 0.5)
    want_r = tile.compact(iota((lanes, CH), 0)).astype(F32)
    spread = one(jnp.where(rank_r == want_r, jnp.broadcast_to(lit, (lanes, CH)), 0.0) > 0.5)
    to_slot = dot(spread, one(slot[...] == ri)).astype(BF16)

    eye = iota((NG, NG), 0) == iota((NG, NG), 1)
    solar = sol[...]
    weight = jnp.sum(jnp.where(eye, solar / jnp.sum(solar, axis=1, keepdims=True), 0.0), axis=1, keepdims=True)
    band_c = jnp.sum(jnp.where(eye, band[...].astype(F32), 0.0), axis=1, keepdims=True)
    k = iota((NG, CH), 1) % 128
    for l8 in range(8):
        pick = one((k // 8).astype(F32) == jnp.where(k % 8 == l8, band_c, -1.0))
        lhs[l8 // 4, (l8 % 4) * NG:(l8 % 4 + 1) * NG, 256:512] = pick
    k4 = iota((NG, CH), 1) - 96
    k4 = jnp.where(k4 >= 56, k4 - 56, k4)
    b4 = jnp.where(iota((NG, CH), 1) < 96, -2.0, (k4 // 4).astype(F32))
    for j in range(4):
        masks[j] = one(iota((16, 128), 1) % 4 == j)
        pick = one(b4 == jnp.where(k4 % 4 == j, band_c, -1.0))
        mixed[j] = pick[:, 0:128]
        for hf in range(2):
            lhs[hf, j * NG:(j + 1) * NG, 128:256] = pick[:, 128:256]

    quarter = iota((8, WIDE), 1) // NARROW

    def pack(get, j):
        if j == 3:
            return jnp.where(quarter == 0, get(24), get(56))
        v = [get(s + 8 * j) for s in STARTS]
        return jnp.where(quarter == 0, v[0], jnp.where(quarter == 1, v[1], jnp.where(quarter == 2, v[2], v[3])))

    cosine = mu[...]
    cos = row_times(cosine, gather)
    cos_safe = jnp.where(cos > 0, cos, 1.0)
    rate = -1.0 / cos_safe
    wfull = jnp.broadcast_to(weight, (NG, WIDE))

    def lanes_of(x, c):
        return x[:, :WIDE] if c < A_CHUNKS else x[:, WIDE:]

    def chunk_of(c, get):
        if c < A_CHUNKS:
            return get(8 * c, 0)
        return pack(lambda row: get(row, WIDE), c - A_CHUNKS)

    def beam_top(c):
        w = chunk_of(c, lambda row, lane: wfull[row:row + 8])
        if c == A_CHUNKS + 3:
            w = jnp.where(quarter < 2, w, 0.0)
        return w * lanes_of(cos, c) * 0.5

    def prepare(grp):
        rows = pl.ds(pl.multiple_of(grp * 8, 8), 8)
        thick = th[rows, :] * (SCALE / NLEV)
        gas = (ab[:, rows, :] * thick[None]).reshape(64, CH)
        tau = (ct[:, rows, :] * SCALE).reshape(112, CH)
        tau_s = tau * cs[:, rows, :].reshape(112, CH)
        tau_f = tau_s * ca[:, rows, :].reshape(112, CH)
        hi, low = halves(jnp.concatenate([gas, tau, tau_s, tau_f], axis=0))
        hi = dot(hi, gather)
        low = dot(low, gather)
        hi_f, low_f = hi, low
        for i in range(2):
            at = 176 + 112 * i
            rhs[256 * i:256 * i + 112] = hi_f[at:at + 112].astype(BF16)
            rhs[256 * i + 128:256 * i + 240] = low_f[at:at + 112].astype(BF16)
        k_rows = kc[:, rows, :].reshape(64, NG)
        k_hi = k_rows.astype(BF16).astype(F32)
        k_low = k_rows - k_hi

        def four(x, count, hf):
            return jnp.concatenate([x[8 * i + 4 * hf:8 * i + 4 * hf + 4] for i in range(count)], axis=0)

        for hf in range(2):
            g_hi, g_low = four(hi_f, 8, hf), four(low_f, 8, hf)
            c_hi, c_low = four(hi_f[64:176], 14, hf), four(low_f[64:176], 14, hf)
            taus[hf] = jnp.concatenate([g_hi, g_low, g_hi, c_hi, c_low, jnp.zeros((48, lanes), F32)], axis=0).astype(BF16)
            kh, kl = four(k_hi, 8, hf), four(k_low, 8, hf)
            k_t = jnp.concatenate([kh, kh, kl, jnp.zeros((32, NG), F32)], axis=0).T.astype(BF16)
            for j in range(4):
                at = j * NG
                lhs[hf, at:at + NG, 0:128] = k_t * jnp.concatenate([masks[j]] * 7, axis=0) + mixed[j]

    for i in range(2):
        rhs[256 * i + 112:256 * i + 128] = jnp.zeros((16, lanes), BF16)
        rhs[256 * i + 240:256 * i + 256] = jnp.zeros((16, lanes), BF16)

    def optics(hf):
        buf[hf, 0] = dot(lhs[hf, :, 0:256], taus[hf])
        buf[hf, 1] = dot(lhs[hf, :, 256:512], rhs[0:256])
        buf[hf, 2] = dot(lhs[hf, :, 256:512], rhs[256:512])

    def descend(grp, hf):
        for c in range(chunks):
            at = slice(8 * c, 8 * c + 8)
            refl, diff, beam = (state[i, at] for i in range(3))
            m, r = lanes_of(cos_safe, c), lanes_of(rate, c)
            for j in range(4):
                t, s, f = (chunk_of(c, lambda row, lane: buf[hf, i, j * NG + row:j * NG + row + 8, lane:lane + WIDE]) for i in range(3))
                p1 = t - s
                p2 = t - f
                pp = p1 * p2
                kk = pp * lax.rsqrt(pp)
                nk2 = kk * -2.0
                e = jnp.exp2(nk2)
                e2 = e * e
                tot = p1 + p2
                inv_d = pl.reciprocal((tot - nk2) - e2 * (tot + nk2), approx=True)
                rdif = (s - f) * (1.0 - e2) * inv_d
                tdif = (kk * 4.0) * e * inv_d
                below = beam * jnp.exp2(t * r)
                sc = (beam - below) * pl.reciprocal(t, approx=True)
                mf = m * f
                s_up = sc * (s - mf)
                s_dn = sc * (s + mf)
                inv = pl.reciprocal(1.0 - rdif * refl, approx=True)
                ti = tdif * inv
                level = pl.multiple_of((grp * 8 + hf * 4 + j) * (8 * chunks), 8) + 8 * c
                w = pl.ds(pl.multiple_of(level, 8), 8)
                coef[0, w] = ti
                coef[1, w] = refl
                coef[2, w] = diff
                coef[3, w] = s_up
                coef[4, w] = rdif * inv
                coef[5, w] = beam
                diff = s_dn + ti * (diff + refl * s_up)
                refl = rdif + tdif * (refl * ti)
                beam = below
            state[0, at] = refl
            state[1, at] = diff
            state[2, at] = beam

    if loaded is not None:
        loaded(0)
    a_hi, a_low = halves(jnp.concatenate([alb[...], jnp.zeros((2, CH), F32)], axis=0))
    zero = jnp.zeros((112, lanes), BF16)
    a_rhs = jnp.concatenate([dot(a_hi, gather).astype(BF16), zero, dot(a_low, gather).astype(BF16), zero], axis=0)
    albs[...] = dot(one(k.astype(F32) == band_c), a_rhs)
    for c in range(chunks):
        at = slice(8 * c, 8 * c + 8)
        state[0, at] = jnp.zeros((8, WIDE), F32)
        state[1, at] = jnp.zeros((8, WIDE), F32)
        state[2, at] = beam_top(c)
    prepare(0)
    optics(0)
    if loaded is not None:
        loaded(1)

    def downward(i, _):
        grp = i
        if midway is not None:
            pl.when(i == 5)(midway)
        optics(1)
        descend(grp, 0)
        prepare(jnp.minimum(grp + 1, 7))
        optics(0)
        descend(grp, 1)
        return 0

    lax.fori_loop(0, 8, downward, 0)

    def side(make):
        parts = [sum(make(c) for c in range(A_CHUNKS))]
        if tile.packed:
            parts.append(sum(make(c) for c in range(A_CHUNKS, chunks)))
        return jnp.concatenate(parts, axis=1)

    flux, ups = [], []
    for c in range(chunks):
        refl, diff, beam = (state[i, 8 * c:8 * c + 8] for i in range(3))
        al = chunk_of(c, lambda row, lane: albs[row:row + 8, lane:lane + WIDE])
        beam = beam + beam
        back = refl * al
        flux.append(beam + (diff + back * beam) * pl.reciprocal(1.0 - back, approx=True))
        ups.append(al * flux[-1])
    surf = jnp.sum(side(lambda c: flux[c]), axis=0, keepdims=True)
    slotted = row_times(surf, to_slot)
    if after_down is not None:
        after_down(slotted)

    net[8 * NLEV:8 * NLEV + 8] = side(lambda c: flux[c] - ups[c])
    UNROLL = 4

    def rise(i, carry):
        up_flux = list(carry)
        for j in range(UNROLL):
            l = NLEV - 1 - (i * UNROLL + j)
            total = [None, None]
            for c in range(chunks):
                w = pl.ds(pl.multiple_of(l * (8 * chunks) + 8 * c, 8), 8)
                ti, refl, diff, s_up, ri, beam = (coef[k, w] for k in range(6))
                up_flux[c] = ti * up_flux[c] + (ri * (diff + refl * s_up) + s_up)
                v = (beam + beam) + ((diff + refl * up_flux[c]) - up_flux[c])
                which = 0 if c < A_CHUNKS else 1
                total[which] = v if total[which] is None else total[which] + v
            at = pl.ds(pl.multiple_of(l * 8, 8), 8)
            net[at, 0:WIDE] = total[0]
            if tile.packed:
                net[at, WIDE:] = total[1]
        return tuple(up_flux)

    lax.fori_loop(0, NLEV // UNROLL, rise, tuple(ups))
    net[8 * 65:8 * 72] = jnp.zeros((56, lanes), F32)
    fl[...] = jnp.sum(net[...].reshape(72, 8, lanes), axis=1)
    hi, mid, low = thirds(fl[0:64] - fl[1:65])
    lost = dot(hi, spread) + dot(mid, spread) + dot(low, spread)
    heat = NLEV * lost / th[...]
    return heat, slotted


def scratch(tile):
    lanes, rows = tile.lanes, 8 * tile.chunks
    return [
        pltpu.VMEM((512, lanes), BF16),
        pltpu.VMEM((2, 256, lanes), BF16),
        pltpu.VMEM((4, 16, 128), BF16),
        pltpu.VMEM((4, NG, 128), BF16),
        pltpu.VMEM((2, 4 * NG, 512), BF16),
        pltpu.VMEM((2, 3, 4 * NG, lanes), F32),
        pltpu.VMEM((3, rows, WIDE), F32),
        pltpu.VMEM((6, NLEV * rows, WIDE), F32),
        pltpu.VMEM((72 * 8, lanes), F32),
        pltpu.VMEM((72, lanes), F32),
        pltpu.VMEM((NG, lanes), F32),
    ]


def overflow_kernel(*refs):
    sun, hbm, outs = refs[0], refs[1:12], refs[12:14]
    local, vals, sem, scr = refs[14:25], refs[25:27], refs[27], refs[28:]

    @pl.when(jnp.sum(jnp.where(sun[...] == 1, 1.0, 0.0)) > MAIN)
    def _():
        for i in range(11):
            copy = pltpu.make_async_copy(hbm[i], local[i], sem.at[i])
            copy.start()
            copy.wait()
        ins = local[:7] + (sun,) + local[7:]
        h, s = physics(Tile(MAIN, False), ins, scr)
        vals[0][...] = h
        vals[1][...] = s
        for i in range(2):
            copy = pltpu.make_async_copy(vals[i], outs[i], sem.at[11 + i])
            copy.start()
            copy.wait()


def main_kernel(*refs):
    big, (mu_hbm, alb_hbm, sun_hbm, slot_hbm, kc_hbm, sol_hbm, band_hbm) = refs[:5], refs[5:12]
    heat0_hbm, slotted0_hbm, (heat, surface) = refs[12], refs[13], refs[14:16]
    send, recv, heat0, send_sem, recv_sem, go, in_sem = refs[16:23]
    local, small, slotted0, scr = refs[23:28], refs[28:35], refs[35], refs[36:]
    mu, alb, sun, slot, kc, sol, band = small
    e, c = lax.axis_index("elem"), lax.axis_index("col")
    me = e * N_COL + c

    def pieces(first):
        got = []
        for i in range(5):
            rows = pl.ds(0, 8) if first else pl.ds(8, NLEV - 8)
            src, dst = (r.at[rows] if i == 4 else r.at[:, rows] for r in (big[i], local[i]))
            got.append(pltpu.make_async_copy(src, dst, in_sem.at[i if first else 5 + i]))
        if first:
            got.append(pltpu.make_async_copy(alb_hbm, alb, in_sem.at[11]))
            got.append(pltpu.make_async_copy(kc_hbm, kc, in_sem.at[12]))
        else:
            got.append(pltpu.make_async_copy(heat0_hbm, heat0, in_sem.at[10]))
            got.append(pltpu.make_async_copy(slotted0_hbm, slotted0, in_sem.at[18]))
        return got

    tiny = [(sun_hbm, sun), (slot_hbm, slot), (mu_hbm, mu), (sol_hbm, sol), (band_hbm, band)]
    tiny = [pltpu.make_async_copy(src, dst, in_sem.at[13 + i]) for i, (src, dst) in enumerate(tiny)]
    for copy in tiny + pieces(True) + pieces(False):
        copy.start()

    barrier = pltpu.get_barrier_semaphore()
    for k in range(1, N_COL):
        pl.semaphore_signal(barrier, inc=1, device_id=(e, lax.rem(c + k, N_COL)), device_id_type=MESH)
    for k in range(1, N_ELEM):
        pl.semaphore_signal(barrier, inc=1, device_id=(lax.rem(e + k, N_ELEM), c), device_id_type=MESH)

    def loaded(part):
        for copy in pieces(part == 0):
            copy.wait()

    def midway():
        pl.semaphore_wait(barrier, N_COL - 1 + N_ELEM - 1)
        for k in range(1, N_ELEM):
            pl.semaphore_signal(go, inc=1, device_id=(lax.rem(e + k, N_ELEM), c), device_id_type=MESH)

    for copy in tiny:
        copy.wait()
    many = jnp.sum(jnp.where(sun[...] == 1, 1.0, 0.0), axis=1, keepdims=True) > MAIN

    def ship(slotted):
        slotted = slotted + jnp.where(many, slotted0[...], 0.0)
        at, s = iota((DEVS, CH), 0), iota((DEVS, CH), 1)
        own = jnp.where(s // 2 == at, slotted, 0.0)
        send[...] = (own[:, :128] + own[:, 128:]).reshape(DEVS, 1, 128)
        pl.semaphore_wait(go, N_ELEM - 1)
        for te, tc in farthest_first(e, c):
            pltpu.make_async_remote_copy(
                src_ref=send.at[te * N_COL + tc],
                dst_ref=recv.at[me],
                send_sem=send_sem,
                recv_sem=recv_sem,
                device_id=(te, tc),
                device_id_type=MESH,
            ).start()
        recv[me] = send[me]

    h, _ = physics(Tile(0, True), local + small, scr, loaded=loaded, midway=midway, after_down=ship)
    heat[...] = h + jnp.where(many, heat0[...], 0.0)
    rest = recv.at[pl.ds(0, DEVS - 1)]
    pltpu.make_async_copy(rest, rest, recv_sem).wait()
    got = recv[...].reshape(DEVS, 128)
    lane = iota((DEVS, 128), 1)
    first = lax.rem(2 * me, 128)
    even = jnp.sum(jnp.where(lane == first, got, 0.0), axis=1, keepdims=True)
    odd = jnp.sum(jnp.where(lane == first + 1, got, 0.0), axis=1, keepdims=True)
    at, s = iota((DEVS, CH), 0), iota((DEVS, CH), 1)
    surface[...] = jnp.sum(jnp.where(s // 2 == at, jnp.where(s % 2 == 0, even, odd), 0.0), axis=0, keepdims=True)
    pltpu.make_async_copy(rest, rest, send_sem).wait()


def store_kernel(heat, surface, heat_out, surface_out, sem):
    copies = [pltpu.make_async_copy(heat, heat_out, sem.at[0]), pltpu.make_async_copy(surface, surface_out, sem.at[1])]
    for copy in copies:
        copy.start()
    for copy in copies:
        copy.wait()


def farthest_first(e, c):
    y, core, x, z = e // 2, lax.rem(e, 2), c // 4, lax.rem(c, 4)
    ys = [lax.rem(y + i, 4) * 2 for i in range(4)]
    cores = [core, 1 - core]
    xs = [lax.rem(x + i, 4) * 4 for i in range(4)]
    zs = [lax.rem(z + i, 4) for i in range(4)]
    elems = {(i, j): ys[i] + cores[j] for i in range(4) for j in range(2)}
    cols = {(i, j): xs[i] + zs[j] for i in range(4) for j in range(4)}
    hops = (0, 1, 2, 1)
    steps = [(i, j, k, m) for i in range(4) for j in range(2) for k in range(4) for m in range(4)][1:]
    steps.sort(key=lambda d: (-(hops[d[0]] + hops[d[2]] + hops[d[3]]), -d[1]))
    return [(elems[d[0], d[1]], cols[d[2], d[3]]) for d in steps]


def body(*args):
    args = tuple(a.reshape(1, -1) if a.ndim == 1 else a for a in args)
    vmem, hbm = pl.BlockSpec(memory_space=pltpu.VMEM), pl.BlockSpec(memory_space=pltpu.HBM)
    outs = (jax.ShapeDtypeStruct((NLEV, CH), F32), jax.ShapeDtypeStruct((1, CH), F32))
    rest = args[:7] + args[8:]
    extra = pl.pallas_call(
        overflow_kernel,
        out_shape=outs,
        in_specs=[vmem] + [hbm] * 11,
        out_specs=(hbm, hbm),
        scratch_shapes=[pltpu.VMEM(a.shape, a.dtype) for a in rest]
        + [pltpu.VMEM((NLEV, CH), F32), pltpu.VMEM((1, CH), F32), pltpu.SemaphoreType.DMA((13,))]
        + scratch(Tile(MAIN, False)),
        compiler_params=pltpu.CompilerParams(vmem_limit_bytes=LIMIT),
    )(args[7], *rest)
    heat, surface = pl.pallas_call(
        main_kernel,
        out_shape=(pltpu.VMEM((NLEV, CH), F32), pltpu.VMEM((1, CH), F32)),
        in_specs=[hbm] * 14,
        out_specs=(vmem, vmem),
        scratch_shapes=[
            pltpu.VMEM((DEVS, 1, 128), F32),
            pltpu.VMEM((DEVS, 1, 128), F32),
            pltpu.VMEM((NLEV, CH), F32),
            pltpu.SemaphoreType.DMA,
            pltpu.SemaphoreType.DMA,
            pltpu.SemaphoreType.REGULAR,
            pltpu.SemaphoreType.DMA((19,)),
        ]
        + [pltpu.VMEM(a.shape, a.dtype) for a in args]
        + [pltpu.VMEM((1, CH), F32)]
        + scratch(Tile(0, True)),
        compiler_params=pltpu.CompilerParams(vmem_limit_bytes=LIMIT, collective_id=0, has_side_effects=True),
    )(*args, *extra)
    heat, surface = pl.pallas_call(
        store_kernel,
        out_shape=outs,
        in_specs=[vmem, vmem],
        out_specs=(hbm, hbm),
        scratch_shapes=[pltpu.SemaphoreType.DMA((2,))],
        compiler_params=pltpu.CompilerParams(vmem_limit_bytes=2 * 2**20),
    )(heat, surface)
    return heat, surface.reshape(CH)


def solution(mesh):
    columns = ("elem", "col")
    return jax.shard_map(
        body,
        mesh=mesh,
        in_specs=(
            P(None, None, columns),
            P(None, None, columns),
            P(None, None, columns),
            P(None, None, columns),
            P(None, columns),
            P(columns),
            P(None, columns),
            P(columns),
            P(columns, None),
            P(),
            P(),
            P(),
        ),
        out_specs=(P(None, columns), P(columns)),
        check_vma=False,
    )
```

```python
import functools
import math

import jax
import jax.numpy as jnp
from jax import lax
from jax.experimental import pallas as pl
from jax.experimental.pallas import tpu as pltpu
from jax.sharding import PartitionSpec as P

MESH = pl.DeviceIdType.MESH
F32 = jnp.float32
BF16 = jnp.bfloat16

NG = 112
NBND = 14
NSP = 8
NLEV = 64
CH = 256
N_ELEM = 8
N_COL = 16
DEVS = 128

WIDE = 128
NARROW = 32
MAIN = WIDE + NARROW
STARTS = (0, 32, 64, 88)
A_CHUNKS = NG // 8
B_CHUNKS = 4
SCALE = math.log2(math.e)


LIMIT = 56 * 2**20


def dot(a, b):
    return jnp.dot(a, b, preferred_element_type=F32)


def iota(shape, axis):
    return lax.broadcasted_iota(jnp.int32, shape, axis)


def one(mask):
    return jnp.where(mask, 1.0, 0.0).astype(BF16)


def halves(x):
    hi = x.astype(BF16)
    return hi, (x - hi.astype(F32)).astype(BF16)


def thirds(x):
    hi = x.astype(BF16)
    rest = x - hi.astype(F32)
    mid = rest.astype(BF16)
    return hi, mid, (rest - mid.astype(F32)).astype(BF16)


def row_times(row, matrix):
    hi, mid, low = thirds(row)
    at = iota((16, row.shape[1]), 0)
    stack = jnp.where(at == 0, hi.astype(F32), jnp.where(at == 1, mid.astype(F32), jnp.where(at == 2, low.astype(F32), 0.0)))
    return jnp.sum(dot(stack.astype(BF16), matrix), axis=0, keepdims=True)


class Tile:
    def __init__(self, first, packed):
        self.first = first
        self.packed = packed
        self.lanes = 2 * WIDE if packed else WIDE
        self.chunks = A_CHUNKS + (B_CHUNKS if packed else 0)

    def compact(self, lane):
        return self.first + jnp.where(lane < WIDE, lane, WIDE + lane % NARROW)


def physics(tile, refs, scr, loaded=None, midway=None, after_down=None):
    (ab, ct, cs, ca, th, mu, alb, sun, slot, kc, sol, band) = refs
    (rhs, taus, masks, mixed, lhs, buf, state, coef, net, fl, albs) = scr
    lanes, chunks = tile.lanes, tile.chunks

    lit = jnp.where(sun[...] == 1, 1.0, 0.0)
    ri, ci = iota((CH, CH), 0), iota((CH, CH), 1)
    litb = jnp.broadcast_to(lit, (CH, CH))
    ones = jnp.ones((CH, CH), BF16)
    rank_c = dot(jnp.where(ci < ri, litb, 0.0).astype(BF16), ones[:, :lanes])
    lit_c = dot(jnp.where(ci == ri, litb, 0.0).astype(BF16), ones[:, :lanes])
    row_lit = jnp.broadcast_to(lit, (16, CH)).astype(BF16)
    rank_r = dot(row_lit, one(ri < ci))[0:1]
    count = dot(row_lit, ones)[0:1]
    want_c = tile.compact(iota((CH, lanes), 1)).astype(F32)
    gather = one(jnp.where(want_c >= count[:, :lanes], jnp.where(iota((CH, lanes), 0) == 0, 1.0, 0.0), jnp.where(rank_c == want_c, lit_c, 0.0)) > 0.5)
    want_r = tile.compact(iota((lanes, CH), 0)).astype(F32)
    spread = one(jnp.where(rank_r == want_r, jnp.broadcast_to(lit, (lanes, CH)), 0.0) > 0.5)
    to_slot = dot(spread, one(slot[...] == ri)).astype(BF16)

    eye = iota((NG, NG), 0) == iota((NG, NG), 1)
    solar = sol[...]
    weight = jnp.sum(jnp.where(eye, solar / jnp.sum(solar, axis=1, keepdims=True), 0.0), axis=1, keepdims=True)
    band_c = jnp.sum(jnp.where(eye, band[...].astype(F32), 0.0), axis=1, keepdims=True)
    k = iota((NG, CH), 1) % 128
    for l8 in range(8):
        pick = one((k // 8).astype(F32) == jnp.where(k % 8 == l8, band_c, -1.0))
        lhs[l8 // 4, (l8 % 4) * NG:(l8 % 4 + 1) * NG, 256:512] = pick
    k4 = iota((NG, CH), 1) - 96
    k4 = jnp.where(k4 >= 56, k4 - 56, k4)
    b4 = jnp.where(iota((NG, CH), 1) < 96, -2.0, (k4 // 4).astype(F32))
    for j in range(4):
        masks[j] = one(iota((16, 128), 1) % 4 == j)
        pick = one(b4 == jnp.where(k4 % 4 == j, band_c, -1.0))
        mixed[j] = pick[:, 0:128]
        for hf in range(2):
            lhs[hf, j * NG:(j + 1) * NG, 128:256] = pick[:, 128:256]

    quarter = iota((8, WIDE), 1) // NARROW

    def pack(get, j):
        if j == 3:
            return jnp.where(quarter == 0, get(24), get(56))
        v = [get(s + 8 * j) for s in STARTS]
        return jnp.where(quarter == 0, v[0], jnp.where(quarter == 1, v[1], jnp.where(quarter == 2, v[2], v[3])))

    cosine = mu[...]
    cos = row_times(cosine, gather)
    cos_safe = jnp.where(cos > 0, cos, 1.0)
    rate = -1.0 / cos_safe
    wfull = jnp.broadcast_to(weight, (NG, WIDE))

    def lanes_of(x, c):
        return x[:, :WIDE] if c < A_CHUNKS else x[:, WIDE:]

    def chunk_of(c, get):
        if c < A_CHUNKS:
            return get(8 * c, 0)
        return pack(lambda row: get(row, WIDE), c - A_CHUNKS)

    def beam_top(c):
        w = chunk_of(c, lambda row, lane: wfull[row:row + 8])
        if c == A_CHUNKS + 3:
            w = jnp.where(quarter < 2, w, 0.0)
        return w * lanes_of(cos, c) * 0.5

    def prepare(grp):
        rows = pl.ds(pl.multiple_of(grp * 8, 8), 8)
        thick = th[rows, :] * (SCALE / NLEV)
        gas = (ab[:, rows, :] * thick[None]).reshape(64, CH)
        tau = (ct[:, rows, :] * SCALE).reshape(112, CH)
        tau_s = tau * cs[:, rows, :].reshape(112, CH)
        tau_f = tau_s * ca[:, rows, :].reshape(112, CH)
        hi, low = halves(jnp.concatenate([gas, tau, tau_s, tau_f], axis=0))
        hi = dot(hi, gather)
        low = dot(low, gather)
        hi_f, low_f = hi, low
        for i in range(2):
            at = 176 + 112 * i
            rhs[256 * i:256 * i + 112] = hi_f[at:at + 112].astype(BF16)
            rhs[256 * i + 128:256 * i + 240] = low_f[at:at + 112].astype(BF16)
        k_rows = kc[:, rows, :].reshape(64, NG)
        k_hi = k_rows.astype(BF16).astype(F32)
        k_low = k_rows - k_hi

        def four(x, count, hf):
            return jnp.concatenate([x[8 * i + 4 * hf:8 * i + 4 * hf + 4] for i in range(count)], axis=0)

        for hf in range(2):
            g_hi, g_low = four(hi_f, 8, hf), four(low_f, 8, hf)
            c_hi, c_low = four(hi_f[64:176], 14, hf), four(low_f[64:176], 14, hf)
            taus[hf] = jnp.concatenate([g_hi, g_low, g_hi, c_hi, c_low, jnp.zeros((48, lanes), F32)], axis=0).astype(BF16)
            kh, kl = four(k_hi, 8, hf), four(k_low, 8, hf)
            k_t = jnp.concatenate([kh, kh, kl, jnp.zeros((32, NG), F32)], axis=0).T.astype(BF16)
            for j in range(4):
                at = j * NG
                lhs[hf, at:at + NG, 0:128] = k_t * jnp.concatenate([masks[j]] * 7, axis=0) + mixed[j]

    for i in range(2):
        rhs[256 * i + 112:256 * i + 128] = jnp.zeros((16, lanes), BF16)
        rhs[256 * i + 240:256 * i + 256] = jnp.zeros((16, lanes), BF16)

    def optics(hf):
        buf[hf, 0] = dot(lhs[hf, :, 0:256], taus[hf])
        buf[hf, 1] = dot(lhs[hf, :, 256:512], rhs[0:256])
        buf[hf, 2] = dot(lhs[hf, :, 256:512], rhs[256:512])

    def descend(grp, hf):
        for c in range(chunks):
            at = slice(8 * c, 8 * c + 8)
            refl, diff, beam = (state[i, at] for i in range(3))
            m, r = lanes_of(cos_safe, c), lanes_of(rate, c)
            for j in range(4):
                t, s, f = (chunk_of(c, lambda row, lane: buf[hf, i, j * NG + row:j * NG + row + 8, lane:lane + WIDE]) for i in range(3))
                p1 = t - s
                p2 = t - f
                pp = p1 * p2
                kk = pp * lax.rsqrt(pp)
                nk2 = kk * -2.0
                e = jnp.exp2(nk2)
                e2 = e * e
                tot = p1 + p2
                inv_d = pl.reciprocal((tot - nk2) - e2 * (tot + nk2), approx=True)
                rdif = (s - f) * (1.0 - e2) * inv_d
                tdif = (kk * 4.0) * e * inv_d
                below = beam * jnp.exp2(t * r)
                sc = (beam - below) * pl.reciprocal(t, approx=True)
                mf = m * f
                s_up = sc * (s - mf)
                s_dn = sc * (s + mf)
                inv = pl.reciprocal(1.0 - rdif * refl, approx=True)
                ti = tdif * inv
                level = pl.multiple_of((grp * 8 + hf * 4 + j) * (8 * chunks), 8) + 8 * c
                w = pl.ds(pl.multiple_of(level, 8), 8)
                coef[0, w] = ti
                coef[1, w] = refl
                coef[2, w] = diff
                coef[3, w] = s_up
                coef[4, w] = rdif * inv
                coef[5, w] = beam
                diff = s_dn + ti * (diff + refl * s_up)
                refl = rdif + tdif * (refl * ti)
                beam = below
            state[0, at] = refl
            state[1, at] = diff
            state[2, at] = beam

    if loaded is not None:
        loaded(0)
    a_hi, a_low = halves(jnp.concatenate([alb[...], jnp.zeros((2, CH), F32)], axis=0))
    zero = jnp.zeros((112, lanes), BF16)
    a_rhs = jnp.concatenate([dot(a_hi, gather).astype(BF16), zero, dot(a_low, gather).astype(BF16), zero], axis=0)
    albs[...] = dot(one(k.astype(F32) == band_c), a_rhs)
    for c in range(chunks):
        at = slice(8 * c, 8 * c + 8)
        state[0, at] = jnp.zeros((8, WIDE), F32)
        state[1, at] = jnp.zeros((8, WIDE), F32)
        state[2, at] = beam_top(c)
    prepare(0)
    optics(0)
    if loaded is not None:
        loaded(1)

    def downward(i, _):
        grp = i
        if midway is not None:
            pl.when(i == 5)(midway)
        optics(1)
        descend(grp, 0)
        prepare(grp + 1)
        optics(0)
        descend(grp, 1)
        return 0

    lax.fori_loop(0, 7, downward, 0)
    optics(1)
    descend(7, 0)
    descend(7, 1)

    def side(make):
        parts = [sum(make(c) for c in range(A_CHUNKS))]
        if tile.packed:
            parts.append(sum(make(c) for c in range(A_CHUNKS, chunks)))
        return jnp.concatenate(parts, axis=1)

    flux, ups = [], []
    for c in range(chunks):
        refl, diff, beam = (state[i, 8 * c:8 * c + 8] for i in range(3))
        al = chunk_of(c, lambda row, lane: albs[row:row + 8, lane:lane + WIDE])
        beam = beam + beam
        back = refl * al
        flux.append(beam + (diff + back * beam) * pl.reciprocal(1.0 - back, approx=True))
        ups.append(al * flux[-1])
    surf = jnp.sum(side(lambda c: flux[c]), axis=0, keepdims=True)
    slotted = row_times(surf, to_slot)
    if after_down is not None:
        after_down(slotted)

    net[8 * NLEV:8 * NLEV + 8] = side(lambda c: flux[c] - ups[c])
    UNROLL = 4

    def rise(i, carry):
        up_flux = list(carry)
        for j in range(UNROLL):
            l = NLEV - 1 - (i * UNROLL + j)
            total = [None, None]
            for c in range(chunks):
                w = pl.ds(pl.multiple_of(l * (8 * chunks) + 8 * c, 8), 8)
                ti, refl, diff, s_up, ri, beam = (coef[k, w] for k in range(6))
                up_flux[c] = ti * up_flux[c] + (ri * (diff + refl * s_up) + s_up)
                v = (beam + beam) + ((diff + refl * up_flux[c]) - up_flux[c])
                which = 0 if c < A_CHUNKS else 1
                total[which] = v if total[which] is None else total[which] + v
            at = pl.ds(pl.multiple_of(l * 8, 8), 8)
            net[at, 0:WIDE] = total[0]
            if tile.packed:
                net[at, WIDE:] = total[1]
        return tuple(up_flux)

    lax.fori_loop(0, NLEV // UNROLL, rise, tuple(ups))
    net[8 * 65:8 * 72] = jnp.zeros((56, lanes), F32)
    fl[...] = jnp.sum(net[...].reshape(72, 8, lanes), axis=1)
    hi, mid, low = thirds(fl[0:64] - fl[1:65])
    lost = dot(hi, spread) + dot(mid, spread) + dot(low, spread)
    heat = NLEV * lost / th[...]
    return heat, slotted


def scratch(tile):
    lanes, rows = tile.lanes, 8 * tile.chunks
    return [
        pltpu.VMEM((512, lanes), BF16),
        pltpu.VMEM((2, 256, lanes), BF16),
        pltpu.VMEM((4, 16, 128), BF16),
        pltpu.VMEM((4, NG, 128), BF16),
        pltpu.VMEM((2, 4 * NG, 512), BF16),
        pltpu.VMEM((2, 3, 4 * NG, lanes), F32),
        pltpu.VMEM((3, rows, WIDE), F32),
        pltpu.VMEM((6, NLEV * rows, WIDE), F32),
        pltpu.VMEM((72 * 8, lanes), F32),
        pltpu.VMEM((72, lanes), F32),
        pltpu.VMEM((NG, lanes), F32),
    ]


def overflow_kernel(*refs):
    sun, hbm, outs = refs[0], refs[1:12], refs[12:14]
    local, vals, sem, scr = refs[14:25], refs[25:27], refs[27], refs[28:]

    @pl.when(jnp.sum(jnp.where(sun[...] == 1, 1.0, 0.0)) > MAIN)
    def _():
        for i in range(11):
            copy = pltpu.make_async_copy(hbm[i], local[i], sem.at[i])
            copy.start()
            copy.wait()
        ins = local[:7] + (sun,) + local[7:]
        h, s = physics(Tile(MAIN, False), ins, scr)
        vals[0][...] = h
        vals[1][...] = s
        for i in range(2):
            copy = pltpu.make_async_copy(vals[i], outs[i], sem.at[11 + i])
            copy.start()
            copy.wait()


def main_kernel(*refs):
    big, (mu_hbm, alb_hbm, sun_hbm, slot_hbm, kc_hbm, sol_hbm, band_hbm) = refs[:5], refs[5:12]
    heat0_hbm, slotted0_hbm, (heat, surface) = refs[12], refs[13], refs[14:16]
    send, recv, heat0, send_sem, recv_sem, go, in_sem = refs[16:23]
    local, small, slotted0, scr = refs[23:28], refs[28:35], refs[35], refs[36:]
    mu, alb, sun, slot, kc, sol, band = small
    e, c = lax.axis_index("elem"), lax.axis_index("col")
    me = e * N_COL + c

    def pieces(first):
        got = []
        for i in range(5):
            rows = pl.ds(0, 8) if first else pl.ds(8, NLEV - 8)
            src, dst = (r.at[rows] if i == 4 else r.at[:, rows] for r in (big[i], local[i]))
            got.append(pltpu.make_async_copy(src, dst, in_sem.at[i if first else 5 + i]))
        if first:
            got.append(pltpu.make_async_copy(alb_hbm, alb, in_sem.at[11]))
            got.append(pltpu.make_async_copy(kc_hbm, kc, in_sem.at[12]))
        else:
            got.append(pltpu.make_async_copy(heat0_hbm, heat0, in_sem.at[10]))
            got.append(pltpu.make_async_copy(slotted0_hbm, slotted0, in_sem.at[18]))
        return got

    tiny = [(sun_hbm, sun), (slot_hbm, slot), (mu_hbm, mu), (sol_hbm, sol), (band_hbm, band)]
    tiny = [pltpu.make_async_copy(src, dst, in_sem.at[13 + i]) for i, (src, dst) in enumerate(tiny)]
    for copy in tiny + pieces(True) + pieces(False):
        copy.start()

    barrier = pltpu.get_barrier_semaphore()
    for k in range(1, N_COL):
        pl.semaphore_signal(barrier, inc=1, device_id=(e, lax.rem(c + k, N_COL)), device_id_type=MESH)
    for k in range(1, N_ELEM):
        pl.semaphore_signal(barrier, inc=1, device_id=(lax.rem(e + k, N_ELEM), c), device_id_type=MESH)

    def loaded(part):
        for copy in pieces(part == 0):
            copy.wait()

    def midway():
        pl.semaphore_wait(barrier, N_COL - 1 + N_ELEM - 1)
        for k in range(1, N_ELEM):
            pl.semaphore_signal(go, inc=1, device_id=(lax.rem(e + k, N_ELEM), c), device_id_type=MESH)

    for copy in tiny:
        copy.wait()
    many = jnp.sum(jnp.where(sun[...] == 1, 1.0, 0.0), axis=1, keepdims=True) > MAIN

    def ship(slotted):
        slotted = slotted + jnp.where(many, slotted0[...], 0.0)
        at, s = iota((DEVS, CH), 0), iota((DEVS, CH), 1)
        own = jnp.where(s // 2 == at, slotted, 0.0)
        send[...] = (own[:, :128] + own[:, 128:]).reshape(DEVS, 1, 128)
        pl.semaphore_wait(go, N_ELEM - 1)
        for te, tc in farthest_first(e, c):
            pltpu.make_async_remote_copy(
                src_ref=send.at[te * N_COL + tc],
                dst_ref=recv.at[me],
                send_sem=send_sem,
                recv_sem=recv_sem,
                device_id=(te, tc),
                device_id_type=MESH,
            ).start()
        recv[me] = send[me]

    h, _ = physics(Tile(0, True), local + small, scr, loaded=loaded, midway=midway, after_down=ship)
    heat[...] = h + jnp.where(many, heat0[...], 0.0)
    rest = recv.at[pl.ds(0, DEVS - 1)]
    pltpu.make_async_copy(rest, rest, recv_sem).wait()
    got = recv[...].reshape(DEVS, 128)
    lane = iota((DEVS, 128), 1)
    first = lax.rem(2 * me, 128)
    even = jnp.sum(jnp.where(lane == first, got, 0.0), axis=1, keepdims=True)
    odd = jnp.sum(jnp.where(lane == first + 1, got, 0.0), axis=1, keepdims=True)
    at, s = iota((DEVS, CH), 0), iota((DEVS, CH), 1)
    surface[...] = jnp.sum(jnp.where(s // 2 == at, jnp.where(s % 2 == 0, even, odd), 0.0), axis=0, keepdims=True)
    pltpu.make_async_copy(rest, rest, send_sem).wait()


def store_kernel(heat, surface, heat_out, surface_out, sem):
    copies = [pltpu.make_async_copy(heat, heat_out, sem.at[0]), pltpu.make_async_copy(surface, surface_out, sem.at[1])]
    for copy in copies:
        copy.start()
    for copy in copies:
        copy.wait()


def farthest_first(e, c):
    y, core, x, z = e // 2, lax.rem(e, 2), c // 4, lax.rem(c, 4)
    ys = [lax.rem(y + i, 4) * 2 for i in range(4)]
    cores = [core, 1 - core]
    xs = [lax.rem(x + i, 4) * 4 for i in range(4)]
    zs = [lax.rem(z + i, 4) for i in range(4)]
    elems = {(i, j): ys[i] + cores[j] for i in range(4) for j in range(2)}
    cols = {(i, j): xs[i] + zs[j] for i in range(4) for j in range(4)}
    hops = (0, 1, 2, 1)
    steps = [(i, j, k, m) for i in range(4) for j in range(2) for k in range(4) for m in range(4)][1:]
    steps.sort(key=lambda d: (-(hops[d[0]] + hops[d[2]] + hops[d[3]]), -d[1]))
    return [(elems[d[0], d[1]], cols[d[2], d[3]]) for d in steps]


def body(*args):
    args = tuple(a.reshape(1, -1) if a.ndim == 1 else a for a in args)
    vmem, hbm = pl.BlockSpec(memory_space=pltpu.VMEM), pl.BlockSpec(memory_space=pltpu.HBM)
    outs = (jax.ShapeDtypeStruct((NLEV, CH), F32), jax.ShapeDtypeStruct((1, CH), F32))
    rest = args[:7] + args[8:]
    extra = pl.pallas_call(
        overflow_kernel,
        out_shape=outs,
        in_specs=[vmem] + [hbm] * 11,
        out_specs=(hbm, hbm),
        scratch_shapes=[pltpu.VMEM(a.shape, a.dtype) for a in rest]
        + [pltpu.VMEM((NLEV, CH), F32), pltpu.VMEM((1, CH), F32), pltpu.SemaphoreType.DMA((13,))]
        + scratch(Tile(MAIN, False)),
        compiler_params=pltpu.CompilerParams(vmem_limit_bytes=LIMIT),
    )(args[7], *rest)
    heat, surface = pl.pallas_call(
        main_kernel,
        out_shape=(pltpu.VMEM((NLEV, CH), F32), pltpu.VMEM((1, CH), F32)),
        in_specs=[hbm] * 14,
        out_specs=(vmem, vmem),
        scratch_shapes=[
            pltpu.VMEM((DEVS, 1, 128), F32),
            pltpu.VMEM((DEVS, 1, 128), F32),
            pltpu.VMEM((NLEV, CH), F32),
            pltpu.SemaphoreType.DMA,
            pltpu.SemaphoreType.DMA,
            pltpu.SemaphoreType.REGULAR,
            pltpu.SemaphoreType.DMA((19,)),
        ]
        + [pltpu.VMEM(a.shape, a.dtype) for a in args]
        + [pltpu.VMEM((1, CH), F32)]
        + scratch(Tile(0, True)),
        compiler_params=pltpu.CompilerParams(vmem_limit_bytes=LIMIT, collective_id=0, has_side_effects=True),
    )(*args, *extra)
    heat, surface = pl.pallas_call(
        store_kernel,
        out_shape=outs,
        in_specs=[vmem, vmem],
        out_specs=(hbm, hbm),
        scratch_shapes=[pltpu.SemaphoreType.DMA((2,))],
        compiler_params=pltpu.CompilerParams(vmem_limit_bytes=2 * 2**20),
    )(heat, surface)
    return heat, surface.reshape(CH)


def solution(mesh):
    columns = ("elem", "col")
    return jax.shard_map(
        body,
        mesh=mesh,
        in_specs=(
            P(None, None, columns),
            P(None, None, columns),
            P(None, None, columns),
            P(None, None, columns),
            P(None, columns),
            P(columns),
            P(None, columns),
            P(columns),
            P(columns, None),
            P(),
            P(),
            P(),
        ),
        out_specs=(P(None, columns), P(columns)),
        check_vma=False,
    )
```
